32 devices in a mesh: walker: 4 (over y, x), tangent: 4 (over z), feat: 2 (over core).
Axes of the slice: x: 2, y: 2, z: 4, core: 2. Of those that a mesh axis runs over, the one named last changes fastest.
Arguments:
- value_in: bfloat16 [128, 512], P('walker', 'feat'), may hold values from -0.94921875 to 0.94921875
- tang_in: bfloat16 [128, 768, 512], P('walker', 'tangent', 'feat'), may hold values from -1.01 to 1.01
- lap_in: bfloat16 [128, 512], P('walker', 'feat'), may hold values from -6 to 6
- w_first: bfloat16 [512, 512], P(('walker', 'tangent', 'feat')), may hold values from -0.25 to 0.25
- b_first: float32 [512], replicated, may hold values from -3 to 3
- w_second: bfloat16 [512, 512], P(('walker', 'tangent', 'feat')), may hold values from -0.25 to 0.25
- b_second: float32 [512], replicated, may hold values from -3 to 3
- readout: float32 [512], replicated, may hold values from -0.6 to 0.6
Outputs:
- log_amplitude: float32 [128], P('walker')
- gradient: float32 [128, 768], P('walker', 'tangent')
- kinetic: float32 [128], P('walker')
The draws below stay inside these ranges and needn't reach their ends.
All inputs are finite; a program needn't handle non-finite values.
Results may differ from the reference program's by a relative error of at most 0.0044.
Values may be sent and summed in bfloat16 or wider, within the bound.
A program may use at most 64 MiB of HBM per device.

```python
import math
import jax
import jax.numpy as jnp
from jax import lax

D = 512
W_DEV = 32
TANGENTS = 768
WALKERS = 128


def draw_tang_in(key, part):
    first_key, second_key = jax.random.split(key, 2)
    columns = jnp.arange(TANGENTS, dtype=jnp.float32)
    growth = jnp.exp(math.log(3.0) * columns / (TANGENTS - 1))[None, :, None]
    spread = jax.random.uniform(second_key, (WALKERS, TANGENTS, 1), minval=0.6, maxval=1.4)
    pattern = jnp.clip(jax.random.normal(first_key, (WALKERS, TANGENTS, D)), -6.0, 6.0)
    return (0.04 * growth * spread * pattern).astype(jnp.bfloat16)


def steps_of(key, extent, cuts, low, top_value):
    def one(position, shards_of):
        draws = jax.random.uniform(jax.random.fold_in(jax.random.fold_in(key, 6), position), (shards_of,), jnp.float32, low / len(cuts), top_value / len(cuts))
        return jnp.repeat(jnp.exp(draws), extent[position] // shards_of).reshape((-1,) + (1,) * (len(extent) - position - 1))

    level = one(*cuts[0])
    for cut in cuts[1:]:
        level = level * one(*cut)
    return level


def normal_values(own_key, shape, scale, most, cuts=(), held_as=jnp.bfloat16):
    loudness = steps_of(own_key, shape, cuts, -0.22, 0.18) if cuts else 1.0
    result = jax.random.normal(own_key, shape, jnp.float32) * scale * loudness
    return jnp.minimum(jnp.maximum(result, -most), most).astype(held_as)


def setup_inputs(seed: int = 0) -> dict:
    arg_keys = jax.random.split(jax.random.key(seed), 9)
    return {
        "value_in": jnp.clip(jax.random.uniform(arg_keys[0], (WALKERS, D), jnp.float32, -0.94921875, 0.94921875) * steps_of(arg_keys[0], (WALKERS, D), ((0, 4), (1, 2)), -0.4, 0.0), -0.94921875, 0.94921875).astype(jnp.bfloat16),
        "tang_in": draw_tang_in(jax.random.fold_in(arg_keys[8], 71), 0),
        "lap_in": normal_values(arg_keys[2], (WALKERS, D), 1.0, 6.0, ((0, 4), (1, 2))),
        "w_first": normal_values(arg_keys[3], (D, D), D ** -0.5, 0.25, ((0, 32),)),
        "b_first": normal_values(arg_keys[4], (D,), 0.5, 3.0, (), jnp.float32),
        "w_second": normal_values(arg_keys[5], (D, D), D ** -0.5, 0.25, ((0, 32),)),
        "b_second": normal_values(arg_keys[6], (D,), 0.5, 3.0, (), jnp.float32),
        "readout": normal_values(arg_keys[7], (D,), 0.1, 0.6, (), jnp.float32),
    }


def tanh_layer(value, tangents, laplacian, weight, bias):
    pre_act = jnp.dot(value, weight, preferred_element_type=jnp.float32) + bias
    lap_pre = jnp.dot(laplacian, weight, preferred_element_type=jnp.float32)
    count_w, count_t, width = tangents.shape
    grad_pre = jnp.dot(tangents.reshape(count_w * count_t, width), weight, preferred_element_type=jnp.float32)
    grad_pre = grad_pre.reshape(count_w, count_t, weight.shape[1])
    hidden = jnp.tanh(pre_act)
    slope = 1.0 - hidden * hidden
    bend = -2.0 * hidden * slope
    curvature = jnp.sum(grad_pre * grad_pre, axis=1)
    return hidden, slope, bend, grad_pre, lap_pre, curvature


def reference(value_in, tang_in, lap_in, w_first, b_first, w_second, b_second, readout):
    blocks = WALKERS // W_DEV

    def one_block(inputs):
        value, tangents, laplacian = inputs
        hidden, slope, bend, grad_pre, lap_pre, curvature = tanh_layer(value, tangents, laplacian, w_first, b_first)
        value_two = hidden.astype(jnp.bfloat16)
        tang_two = (slope[:, None, :] * grad_pre).astype(jnp.bfloat16)
        lap_two = (slope * lap_pre + bend * curvature).astype(jnp.bfloat16)
        hidden, slope, bend, grad_pre, lap_pre, curvature = tanh_layer(value_two, tang_two, lap_two, w_second, b_second)
        log_amplitude = jnp.sum(readout * hidden, axis=-1)
        gradient = jnp.sum(grad_pre * (readout * slope)[:, None, :], axis=-1)
        laplace = jnp.sum(readout * (slope * lap_pre + bend * curvature), axis=-1)
        kinetic = -0.5 * (laplace + jnp.sum(gradient * gradient, axis=-1))
        return log_amplitude, gradient, kinetic

    log_amplitude, gradient, kinetic = lax.map(one_block, (value_in.reshape(blocks, W_DEV, D), tang_in.reshape(blocks, W_DEV, TANGENTS, D), lap_in.reshape(blocks, W_DEV, D)))
    return log_amplitude.reshape(WALKERS), gradient.reshape(WALKERS, TANGENTS), kinetic.reshape(WALKERS)
```

```python
import functools

import jax
import jax.numpy as jnp
from jax import lax
from jax.experimental import pallas as pl
from jax.experimental.pallas import tpu as pltpu
from jax.sharding import PartitionSpec as P

F32 = jnp.float32
BF16 = jnp.bfloat16
MESH = pl.DeviceIdType.MESH
CHUNK = 4


def dot(a, b):
    return jnp.dot(a, b, preferred_element_type=F32)


def dot_t(a, b):
    return lax.dot_general(a, b, (((1,), (1,)), ((), ())), preferred_element_type=F32)


def halves(a):
    high = a.astype(BF16)
    low = (a - high.astype(F32)).astype(BF16)
    return jnp.concatenate([high, low], axis=0)


def kernel(
    nw, nz, gather,
    value_ref, tang_ref, lap_ref, w1_ref, b1_ref, w2_ref, b2_ref, r_ref,
    grad_out, small_out,
    x, w1_all, w2_all, vl, vec, slope_s, curv1_s, curv2_s, gbuf, msg, small_s,
    loc, ps, pr, za_s, za_r, wb_s, wb_r, fc_s, fc_r, gs, gr, ms, mr,
):
    w, z, f = lax.axis_index("walker"), lax.axis_index("tangent"), lax.axis_index("feat")
    other = 1 - f
    own, cols, width = x.shape
    half = width // 2
    chunks = own // CHUNK
    mine = pl.ds(pl.multiple_of(f * own, own), own)
    theirs = pl.ds(pl.multiple_of(other * own, own), own)
    my_cols = pl.ds(pl.multiple_of(f * half, half), half)
    their_cols = pl.ds(pl.multiple_of(other * half, half), half)
    partner = (w, z, other)

    def z_at(k):
        return lax.rem(z + k, nz)

    def w_at(k):
        return lax.rem(w + k, nw)

    def remote(src, dst, send, recv, device):
        return pltpu.make_async_remote_copy(
            src_ref=src, dst_ref=dst, send_sem=send, recv_sem=recv, device_id=device, device_id_type=MESH
        )

    local = []

    def fetch(src, dst):
        copy = pltpu.make_async_copy(src, dst, loc.at[len(local)])
        copy.start()
        local.append(copy)
        return copy

    own_w = [
        fetch(src, dst.at[w, z, f] if gather else dst) for src, dst in ((w1_ref, w1_all), (w2_ref, w2_all))
    ]
    own_vec = [fetch(src, vec.at[i]) for i, src in enumerate((b1_ref, b2_ref, r_ref))]
    own_vl = [fetch(src.at[mine, :], vl.at[i, :, my_cols]) for i, src in enumerate((value_ref, lap_ref))]
    own_tang = []
    for c in range(chunks):
        rows = pl.ds(f * own + c * CHUNK, CHUNK)
        own_tang.append(fetch(tang_ref.at[rows], x.at[pl.ds(c * CHUNK, CHUNK), :, my_cols]))

    barrier = pltpu.get_barrier_semaphore()
    greeted = [partner]
    for k in range(1, nz):
        greeted += [(w, z_at(k), f), (w, z_at(k), other)]
    if gather:
        greeted += [(w_at(k), z, f) for k in range(1, nw)]
    for device in greeted:
        pl.semaphore_signal(barrier, inc=1, device_id=device, device_id_type=MESH)
    pl.semaphore_wait(barrier, len(greeted))

    sent = []

    def send(*args):
        copy = remote(*args)
        copy.start()
        sent.append(copy)

    def arrived(ref, send_sem, recv_sem):
        remote(ref, ref, send_sem, recv_sem, partner).wait_recv()

    weights = ((w1_ref, w1_all), (w2_ref, w2_all))

    def along_z(layer):
        src, dst = weights[layer]
        for k in range(1, nz):
            send(src, dst.at[w, z, f], za_s.at[layer, k], za_r.at[layer, k], (w, z_at(k), f))

    def to_partner(layer, k):
        dst = weights[layer][1]
        piece = dst.at[w_at(nw - k), :, f]
        send(piece, piece, fc_s.at[layer, k], fc_r.at[layer, k], partner)

    def across(layer):
        dst = weights[layer][1]
        own_w[layer].wait()
        for k in range(1, nz):
            arrived(dst.at[w, z_at(nz - k), f], za_s.at[layer, k], za_r.at[layer, k])
        piece = dst.at[w, :, f]
        for k in range(1, nw):
            send(piece, piece, wb_s.at[layer, k], wb_r.at[layer, k], (w_at(k), z, f))
        to_partner(layer, 0)

    def relay(layer):
        dst = weights[layer][1]
        for k in range(1, nw):
            arrived(dst.at[w_at(nw - k), :, f], wb_s.at[layer, k], wb_r.at[layer, k])
            to_partner(layer, k)

    def whole(layer):
        dst = weights[layer][1]
        if gather:
            for k in range(nw):
                arrived(dst.at[w_at(nw - k), :, other], fc_s.at[layer, k], fc_r.at[layer, k])
        else:
            own_w[layer].wait()
        return dst[...].reshape(width, width)

    if gather:
        along_z(0)
    for i, src in enumerate((value_ref, lap_ref)):
        send(src.at[theirs, :], vl.at[i, :, my_cols], ps.at[i], pr.at[i], partner)
    for c in range(chunks):
        rows = pl.ds(other * own + c * CHUNK, CHUNK)
        send(
            tang_ref.at[rows], x.at[pl.ds(c * CHUNK, CHUNK), :, my_cols],
            ps.at[2 + c], pr.at[2 + c], partner,
        )
    if gather:
        along_z(1)
        across(0)
        relay(0)
        across(1)

    for copy in own_vec + own_vl + own_tang:
        copy.wait()
    for i in range(2):
        arrived(vl.at[i, :, their_cols], ps.at[i], pr.at[i])
    for c in range(chunks):
        arrived(x.at[pl.ds(c * CHUNK, CHUNK), :, their_cols], ps.at[2 + c], pr.at[2 + c])
    b1, b2, readout = vec[0], vec[1], vec[2]

    w1 = whole(0)
    vl_one = dot(vl[...].reshape(2 * own, width), w1)
    hidden_one = jnp.tanh(vl_one[:own] + b1)
    lapin_one = vl_one[own:]
    slope_one = 1.0 - hidden_one * hidden_one
    bend_one = -2.0 * hidden_one * slope_one
    slope_s[...] = slope_one

    def first(c, carry):
        block = x[pl.ds(c * CHUNK, CHUNK)].reshape(CHUNK * cols, width)
        grad = dot(block, w1)
        for i in range(CHUNK):
            row = c * CHUNK + i
            g = grad[i * cols:(i + 1) * cols]
            curv1_s[pl.ds(row, 1), :] = jnp.sum(g * g, axis=0, keepdims=True)
            x[row] = (slope_s[pl.ds(row, 1), :] * g).astype(BF16)
        return carry

    lax.fori_loop(0, chunks, first, 0)

    if gather:
        relay(1)
    w2 = whole(1)
    hidden_two = jnp.tanh(dot(hidden_one.astype(BF16), w2) + b2)
    slope_two = 1.0 - hidden_two * hidden_two
    bend_two = -2.0 * hidden_two * slope_two
    back = dot_t(halves(readout * slope_two), w2)
    back = back[:own] + back[own:]
    back_terms = halves(back)
    term_row = lax.rem(lax.broadcasted_iota(jnp.int32, (2 * own, cols), 0), own)

    def second(c, carry):
        block = x[pl.ds(c * CHUNK, CHUNK)].reshape(CHUNK * cols, width)
        grad = dot(block, w2)
        for i in range(CHUNK):
            row = c * CHUNK + i
            g = grad[i * cols:(i + 1) * cols]
            curv2_s[pl.ds(row, 1), :] = jnp.sum(g * g, axis=0, keepdims=True)
            terms = dot_t(back_terms, x[row])
            gbuf[pl.ds(row, 1), :] = jnp.sum(jnp.where(term_row == row, terms, 0.0), axis=0, keepdims=True)
        return carry

    lax.fori_loop(0, chunks, second, 0)

    send(gbuf, grad_out.at[mine, :], gs, gr, partner)
    keep = pltpu.make_async_copy(gbuf, grad_out.at[mine, :], loc.at[len(local)])
    keep.start()
    gradient = gbuf[...]
    first_z = z == 0
    once = jnp.sum(back * slope_one * lapin_one, axis=1, keepdims=True)
    part = (
        jnp.sum(readout * bend_two * curv2_s[...] + back * bend_one * curv1_s[...], axis=1, keepdims=True)
        + jnp.sum(gradient * gradient, axis=1, keepdims=True)
        + jnp.where(first_z, once, 0.0)
    )
    amp = jnp.where(first_z, jnp.sum(readout * hidden_two, axis=1, keepdims=True), 0.0)
    lane = lax.broadcasted_iota(jnp.int32, (own, 128), 1)
    place = lane == lax.broadcasted_iota(jnp.int32, (own, 128), 0) + f * own
    kin_row = jnp.sum(jnp.where(place, part, 0.0), axis=0, keepdims=True)
    amp_row = jnp.sum(jnp.where(place, amp, 0.0), axis=0, keepdims=True)
    tile_row = lax.broadcasted_iota(jnp.int32, (8, 128), 0)
    msg[z, f] = jnp.where(tile_row == 0, amp_row, -0.5 * kin_row)
    slot = msg.at[z, f]
    others = [(k, g) for k in range(nz) for g in range(2) if k or g]
    for k, g in others:
        send(slot, slot, ms.at[k, g], mr.at[k, g], (w, z_at(k), other if g else f))
    for k, g in others:
        arrived(msg.at[z_at(nz - k), other if g else f], ms.at[k, g], mr.at[k, g])
    total = msg[0, 0] + msg[0, 1]
    for k in range(1, nz):
        total = total + (msg[k, 0] + msg[k, 1])
    small_s[...] = total
    last = pltpu.make_async_copy(small_s, small_out, loc.at[len(local) + 1])
    last.start()
    arrived(grad_out.at[theirs, :], gs, gr)
    keep.wait()
    last.wait()
    for copy in sent:
        copy.wait_send()


def per_device(nw, nz, value_in, tang_in, lap_in, w_first, b_first, w_second, b_second, readout):
    walkers, cols, half = tang_in.shape
    width, own = 2 * half, walkers // 2
    shard = w_first.shape[0]
    gather = shard % 16 == 0
    if gather:
        w_shape = (nw, nz, 2, shard, width)
    else:
        w_shape = (width, width)
        w_first, w_second = (
            lax.all_gather(a, ("walker", "tangent", "feat"), axis=0, tiled=True) for a in (w_first, w_second)
        )
    chunks = own // CHUNK
    dma = pltpu.SemaphoreType.DMA
    anywhere = pl.BlockSpec(memory_space=pl.ANY)
    rows = own * cols
    grad, small = pl.pallas_call(
        functools.partial(kernel, nw, nz, gather),
        out_shape=(
            jax.ShapeDtypeStruct((walkers, cols), F32),
            jax.ShapeDtypeStruct((8, 128), F32),
        ),
        in_specs=[anywhere] * 8,
        out_specs=(anywhere, anywhere),
        scratch_shapes=[
            pltpu.VMEM((own, cols, width), BF16),
            pltpu.VMEM(w_shape, BF16),
            pltpu.VMEM(w_shape, BF16),
            pltpu.VMEM((2, own, width), BF16),
            pltpu.VMEM((3, 1, width), F32),
            pltpu.VMEM((own, width), F32),
            pltpu.VMEM((own, width), F32),
            pltpu.VMEM((own, width), F32),
            pltpu.VMEM((own, cols), F32),
            pltpu.VMEM((nz, 2, 8, 128), F32),
            pltpu.VMEM((8, 128), F32),
            dma((9 + chunks,)),
            dma((2 + chunks,)),
            dma((2 + chunks,)),
            dma((2, nz)),
            dma((2, nz)),
            dma((2, nw)),
            dma((2, nw)),
            dma((2, nw)),
            dma((2, nw)),
            dma,
            dma,
            dma((nz, 2)),
            dma((nz, 2)),
        ],
        compiler_params=pltpu.CompilerParams(
            collective_id=0, has_side_effects=True, vmem_limit_bytes=50 * 2**20
        ),
        cost_estimate=pl.CostEstimate(
            flops=4 * rows * width * width, bytes_accessed=2 * rows * width, transcendentals=0
        ),
    )(
        value_in, tang_in, lap_in, w_first, b_first.reshape(1, width),
        w_second, b_second.reshape(1, width), readout.reshape(1, width),
    )
    return (small[0, :walkers], grad, small[1, :walkers])


def solution(mesh):
    placed = (
        P("walker", "feat"),
        P("walker", "tangent", "feat"),
        P("walker", "feat"),
        P(("walker", "tangent", "feat"), None),
        P(),
        P(("walker", "tangent", "feat"), None),
        P(),
        P(),
    )
    return jax.shard_map(
        functools.partial(per_device, mesh.shape["walker"], mesh.shape["tangent"]),
        mesh=mesh,
        in_specs=placed,
        out_specs=(P("walker"), P("walker", "tangent"), P("walker")),
        check_vma=False,
    )
```

```python
import functools

import jax
import jax.numpy as jnp
from jax import lax
from jax.experimental import pallas as pl
from jax.experimental.pallas import tpu as pltpu
from jax.sharding import PartitionSpec as P

F32 = jnp.float32
BF16 = jnp.bfloat16
MESH = pl.DeviceIdType.MESH
CHUNK = 4


def dot(a, b):
    return jnp.dot(a, b, preferred_element_type=F32)


def halves(a):
    high = a.astype(BF16)
    low = (a - high.astype(F32)).astype(BF16)
    return jnp.concatenate([high, low], axis=0)


def kernel(
    nw, nz, gather,
    value_ref, tang_ref, lap_ref, w1_ref, b1_ref, w2_ref, b2_ref, r_ref,
    out,
    x, w1_all, w2_all, vl, vec, slope_s, weight_s, curv1_s, curv2_s, msg,
    loc, ps, pr, za_s, za_r, wb_s, wb_r, fc_s, fc_r, gs, gr, ms, mr,
):
    w, z, f = lax.axis_index("walker"), lax.axis_index("tangent"), lax.axis_index("feat")
    other = 1 - f
    own, cols, width = x.shape
    half = width // 2
    chunks = own // CHUNK
    mine = pl.ds(pl.multiple_of(f * own, own), own)
    theirs = pl.ds(pl.multiple_of(other * own, own), own)
    my_cols = pl.ds(pl.multiple_of(f * half, half), half)
    their_cols = pl.ds(pl.multiple_of(other * half, half), half)
    partner = (w, z, other)

    def z_at(k):
        return lax.rem(z + k, nz)

    def w_at(k):
        return lax.rem(w + k, nw)

    def remote(src, dst, send, recv, device):
        return pltpu.make_async_remote_copy(
            src_ref=src, dst_ref=dst, send_sem=send, recv_sem=recv, device_id=device, device_id_type=MESH
        )

    local = []

    def fetch(src, dst):
        copy = pltpu.make_async_copy(src, dst, loc.at[len(local)])
        copy.start()
        local.append(copy)
        return copy

    own_w = [
        fetch(src, dst.at[w, z, f] if gather else dst) for src, dst in ((w1_ref, w1_all), (w2_ref, w2_all))
    ]
    own_vec = [fetch(src, vec.at[i]) for i, src in enumerate((b1_ref, b2_ref, r_ref))]
    own_vl = [fetch(src.at[mine, :], vl.at[i, :, my_cols]) for i, src in enumerate((value_ref, lap_ref))]
    own_tang = []
    for c in range(chunks):
        rows = pl.ds(f * own + c * CHUNK, CHUNK)
        own_tang.append(fetch(tang_ref.at[rows], x.at[pl.ds(c * CHUNK, CHUNK), :, my_cols]))

    barrier = pltpu.get_barrier_semaphore()
    greeted = [partner]
    for k in range(1, nz):
        greeted += [(w, z_at(k), f), (w, z_at(k), other)]
    if gather:
        greeted += [(w_at(k), z, f) for k in range(1, nw)]
    for device in greeted:
        pl.semaphore_signal(barrier, inc=1, device_id=device, device_id_type=MESH)
    pl.semaphore_wait(barrier, len(greeted))

    sent = []

    def send(*args):
        copy = remote(*args)
        copy.start()
        sent.append(copy)

    def arrived(ref, send_sem, recv_sem):
        remote(ref, ref, send_sem, recv_sem, partner).wait_recv()

    weights = ((w1_ref, w1_all), (w2_ref, w2_all))

    def along_z(layer):
        src, dst = weights[layer]
        for k in range(1, nz):
            send(src, dst.at[w, z, f], za_s.at[layer, k], za_r.at[layer, k], (w, z_at(k), f))

    def pass_across(layer, k):
        src, dst = weights[layer]
        piece = dst.at[w, z_at(nz - k), f]
        if k:
            arrived(piece, za_s.at[layer, k], za_r.at[layer, k])
        for j in range(1, nw):
            send(src if k == 0 else piece, piece, wb_s.at[layer, k, j], wb_r.at[layer, k, j], (w_at(j), z, f))

    def pass_over(layer, k):
        dst = weights[layer][1]
        if k == 0:
            own_w[layer].wait()
        for j in range(1, nw):
            arrived(dst.at[w_at(nw - j), z_at(nz - k), f], wb_s.at[layer, k, j], wb_r.at[layer, k, j])
        piece = dst.at[:, z_at(nz - k), f]
        send(piece, piece, fc_s.at[layer, k], fc_r.at[layer, k], partner)

    def whole(layer):
        dst = weights[layer][1]
        if gather:
            for k in range(nz):
                arrived(dst.at[:, z_at(nz - k), other], fc_s.at[layer, k], fc_r.at[layer, k])
        else:
            own_w[layer].wait()
        return dst[...].reshape(width, width)

    if gather:
        along_z(0)
        pass_across(0, 0)
    for i, src in enumerate((value_ref, lap_ref)):
        send(src.at[theirs, :], vl.at[i, :, my_cols], ps.at[i], pr.at[i], partner)
    for c in range(chunks):
        rows = pl.ds(other * own + c * CHUNK, CHUNK)
        send(
            tang_ref.at[rows], x.at[pl.ds(c * CHUNK, CHUNK), :, my_cols],
            ps.at[2 + c], pr.at[2 + c], partner,
        )
    if gather:
        along_z(1)
        for k in range(1, nz):
            pass_across(0, k)
            pass_over(0, k - 1)
        pass_over(0, nz - 1)
        for k in range(nz):
            pass_across(1, k)

    for copy in own_vec + own_vl + own_tang:
        copy.wait()
    for i in range(2):
        arrived(vl.at[i, :, their_cols], ps.at[i], pr.at[i])
    for c in range(chunks):
        arrived(x.at[pl.ds(c * CHUNK, CHUNK), :, their_cols], ps.at[2 + c], pr.at[2 + c])
    b1, b2, readout = vec[0], vec[1], vec[2]

    w1 = whole(0)
    vl_one = dot(vl[...].reshape(2 * own, width), w1)
    hidden_one = jnp.tanh(vl_one[:own] + b1)
    lapin_one = vl_one[own:]
    slope_one = 1.0 - hidden_one * hidden_one
    bend_one = -2.0 * hidden_one * slope_one
    slope_s[...] = slope_one

    def first(c, carry):
        block = x[pl.ds(c * CHUNK, CHUNK)].reshape(CHUNK * cols, width)
        grad = dot(block, w1)
        for i in range(CHUNK):
            row = c * CHUNK + i
            g = grad[i * cols:(i + 1) * cols]
            curv1_s[pl.ds(row, 1), :] = jnp.sum(g * g, axis=0, keepdims=True)
            x[row] = (slope_s[pl.ds(row, 1), :] * g).astype(BF16)
        return carry

    lax.fori_loop(0, chunks - 1, first, 0)
    if gather:
        for k in range(nz):
            pass_over(1, k)
    first(chunks - 1, 0)

    w2 = whole(1)
    first_z = z == 0
    lap_two = bend_one * curv1_s[...] + jnp.where(first_z, slope_one * lapin_one, 0.0)
    vl_two = dot(jnp.concatenate([hidden_one.astype(BF16), halves(lap_two)], axis=0), w2)
    hidden_two = jnp.tanh(vl_two[:own] + b2)
    lapin_two = vl_two[own:2 * own] + vl_two[2 * own:]
    slope_two = 1.0 - hidden_two * hidden_two
    bend_two = -2.0 * hidden_two * slope_two
    weight_s[...] = readout * slope_two

    def second(c, carry):
        block = x[pl.ds(c * CHUNK, CHUNK)].reshape(CHUNK * cols, width)
        grad = dot(block, w2)
        for i in range(CHUNK):
            row = c * CHUNK + i
            g = grad[i * cols:(i + 1) * cols]
            curv2_s[pl.ds(row, 1), :] = jnp.sum(g * g, axis=0, keepdims=True)
            terms = weight_s[pl.ds(row, 1), :] * g
            terms = sum(terms[:, j:j + 128] for j in range(0, width, 128))
            out[pl.ds(f * own + row, 1), 0:cols] = jnp.sum(terms.T, axis=0, keepdims=True)
        return carry

    lax.fori_loop(0, chunks, second, 0)

    send(out.at[mine, :], out.at[mine, :], gs, gr, partner)
    gradient = out[mine, 0:cols]
    part = jnp.sum(
        readout * (slope_two * lapin_two + bend_two * curv2_s[...]), axis=1, keepdims=True
    ) + jnp.sum(gradient * gradient, axis=1, keepdims=True)
    amp = jnp.where(first_z, jnp.sum(readout * hidden_two, axis=1, keepdims=True), 0.0)
    lane = lax.broadcasted_iota(jnp.int32, (own, 128), 1)
    place = lane == lax.broadcasted_iota(jnp.int32, (own, 128), 0) + f * own
    kin_row = jnp.sum(jnp.where(place, part, 0.0), axis=0, keepdims=True)
    amp_row = jnp.sum(jnp.where(place, amp, 0.0), axis=0, keepdims=True)
    tile_row = lax.broadcasted_iota(jnp.int32, (8, 128), 0)
    msg[z, f] = jnp.where(tile_row == 0, amp_row, -0.5 * kin_row)
    slot = msg.at[z, f]
    others = [(k, g) for k in range(nz) for g in range(2) if k or g]
    for k, g in others:
        send(slot, slot, ms.at[k, g], mr.at[k, g], (w, z_at(k), other if g else f))
    for k, g in others:
        arrived(msg.at[z_at(nz - k), other if g else f], ms.at[k, g], mr.at[k, g])
    total = msg[0, 0] + msg[0, 1]
    for k in range(1, nz):
        total = total + (msg[k, 0] + msg[k, 1])
    out[2 * own:2 * own + 8, 0:128] = total
    arrived(out.at[theirs, :], gs, gr)
    for copy in sent:
        copy.wait_send()


def per_device(nw, nz, value_in, tang_in, lap_in, w_first, b_first, w_second, b_second, readout):
    walkers, cols, half = tang_in.shape
    width, own = 2 * half, walkers // 2
    shard = w_first.shape[0]
    gather = shard % 16 == 0
    if gather:
        w_shape = (nw, nz, 2, shard, width)
    else:
        w_shape = (width, width)
        w_first, w_second = (
            lax.all_gather(a, ("walker", "tangent", "feat"), axis=0, tiled=True) for a in (w_first, w_second)
        )
    chunks = own // CHUNK
    dma = pltpu.SemaphoreType.DMA
    in_hbm = pl.BlockSpec(memory_space=pltpu.HBM)
    rows = own * cols
    out = pl.pallas_call(
        functools.partial(kernel, nw, nz, gather),
        out_shape=jax.ShapeDtypeStruct((walkers + 8, cols if cols > 128 else 128), F32),
        in_specs=[in_hbm] * 8,
        out_specs=pl.BlockSpec(memory_space=pltpu.VMEM),
        scratch_shapes=[
            pltpu.VMEM((own, cols, width), BF16),
            pltpu.VMEM(w_shape, BF16),
            pltpu.VMEM(w_shape, BF16),
            pltpu.VMEM((2, own, width), BF16),
            pltpu.VMEM((3, 1, width), F32),
            pltpu.VMEM((own, width), F32),
            pltpu.VMEM((own, width), F32),
            pltpu.VMEM((own, width), F32),
            pltpu.VMEM((own, width), F32),
            pltpu.VMEM((nz, 2, 8, 128), F32),
            dma((7 + chunks,)),
            dma((2 + chunks,)),
            dma((2 + chunks,)),
            dma((2, nz)),
            dma((2, nz)),
            dma((2, nz, nw)),
            dma((2, nz, nw)),
            dma((2, nz)),
            dma((2, nz)),
            dma,
            dma,
            dma((nz, 2)),
            dma((nz, 2)),
        ],
        compiler_params=pltpu.CompilerParams(
            collective_id=0, has_side_effects=True, vmem_limit_bytes=64 * 2**20
        ),
        cost_estimate=pl.CostEstimate(
            flops=4 * rows * width * width, bytes_accessed=2 * rows * width, transcendentals=0
        ),
    )(
        value_in, tang_in, lap_in, w_first, b_first.reshape(1, width),
        w_second, b_second.reshape(1, width), readout.reshape(1, width),
    )
    return (out[walkers, :walkers], out[:walkers, :cols], out[walkers + 1, :walkers])


def solution(mesh):
    placed = (
        P("walker", "feat"),
        P("walker", "tangent", "feat"),
        P("walker", "feat"),
        P(("walker", "tangent", "feat"), None),
        P(),
        P(("walker", "tangent", "feat"), None),
        P(),
        P(),
    )
    return jax.shard_map(
        functools.partial(per_device, mesh.shape["walker"], mesh.shape["tangent"]),
        mesh=mesh,
        in_specs=placed,
        out_specs=(P("walker"), P("walker", "tangent"), P("walker")),
        check_vma=False,
    )
```

```python
import functools

import jax
import jax.numpy as jnp
from jax import lax
from jax.experimental import pallas as pl
from jax.experimental.pallas import tpu as pltpu
from jax.sharding import PartitionSpec as P

F32 = jnp.float32
BF16 = jnp.bfloat16
MESH = pl.DeviceIdType.MESH
CHUNK = 4


def dot(a, b):
    return jnp.dot(a, b, preferred_element_type=F32)


def halves(a):
    high = a.astype(BF16)
    low = (a - high.astype(F32)).astype(BF16)
    return jnp.concatenate([high, low], axis=0)


def kernel(
    nw, nz, gather,
    value_ref, tang_ref, lap_ref, w1_ref, b1_ref, w2_ref, b2_ref, r_ref,
    grad_out, amp_out, kin_out,
    x, w1_all, w2_all, vl, vec, slope_s, weight_s, curv1_s, curv2_s, gbuf, msg,
    loc, ps, pr, za_s, za_r, wb_s, wb_r, fc_s, fc_r, vb_s, vb_r, vc_s, vc_r, gs, gr, ms, mr,
):
    w, z, f = lax.axis_index("walker"), lax.axis_index("tangent"), lax.axis_index("feat")
    other = 1 - f
    own, cols, width = x.shape
    half = width // 2
    chunks = own // CHUNK
    mine = pl.ds(pl.multiple_of(f * own, own), own)
    theirs = pl.ds(pl.multiple_of(other * own, own), own)
    my_cols = pl.ds(pl.multiple_of(f * half, half), half)
    their_cols = pl.ds(pl.multiple_of(other * half, half), half)
    partner = (w, z, other)

    def z_at(k):
        return lax.rem(z + k, nz)

    def w_at(k):
        return lax.rem(w + k, nw)

    def remote(src, dst, send, recv, device):
        return pltpu.make_async_remote_copy(
            src_ref=src, dst_ref=dst, send_sem=send, recv_sem=recv, device_id=device, device_id_type=MESH
        )

    local = []

    def fetch(src, dst):
        copy = pltpu.make_async_copy(src, dst, loc.at[len(local)])
        copy.start()
        local.append(copy)
        return copy

    own_w = [
        fetch(src, dst.at[w, z, f] if gather else dst) for src, dst in ((w1_ref, w1_all), (w2_ref, w2_all))
    ]
    own_vec = [fetch(src, vec.at[i]) for i, src in enumerate((b1_ref, b2_ref, r_ref))]
    own_vl = [fetch(src.at[mine, :], vl.at[i, :, my_cols]) for i, src in enumerate((value_ref, lap_ref))]
    tang_at = len(local)
    for c in range(chunks):
        rows = pl.ds(f * own + c * CHUNK, CHUNK)
        fetch(tang_ref.at[rows], x.at[pl.ds(c * CHUNK, CHUNK), :, my_cols])

    barrier = pltpu.get_barrier_semaphore()
    greeted = [partner]
    for k in range(1, nz):
        greeted += [(w, z_at(k), f), (w, z_at(k), other)]
    if gather:
        greeted += [(w_at(k), z, f) for k in range(1, nw)]
    for device in greeted:
        pl.semaphore_signal(barrier, inc=1, device_id=device, device_id_type=MESH)
    if gather:
        for copy in own_w:
            copy.wait()
    pl.semaphore_wait(barrier, len(greeted))

    sent = []

    def send(*args):
        copy = remote(*args)
        copy.start()
        sent.append(copy)

    def arrived(ref, send_sem, recv_sem):
        remote(ref, ref, send_sem, recv_sem, partner).wait_recv()

    weights = (w1_all, w2_all)

    def along_z(layer):
        piece = weights[layer].at[w, z, f]
        for k in range(1, nz):
            send(piece, piece, za_s.at[layer, k], za_r.at[layer, k], (w, z_at(k), f))

    def from_z(layer, k):
        arrived(weights[layer].at[w, z_at(nz - k), f], za_s.at[layer, k], za_r.at[layer, k])

    def pass_across(k):
        piece = w1_all.at[w, z_at(nz - k), f]
        for j in range(1, nw):
            send(piece, piece, wb_s.at[k, j], wb_r.at[k, j], (w_at(j), z, f))

    def pass_over(k):
        for j in range(1, nw):
            arrived(w1_all.at[w_at(nw - j), z_at(nz - k), f], wb_s.at[k, j], wb_r.at[k, j])
        piece = w1_all.at[:, z_at(nz - k), f]
        send(piece, piece, fc_s.at[k], fc_r.at[k], partner)

    def second_across():
        piece = w2_all.at[w, :, f]
        for j in range(1, nw):
            send(piece, piece, vb_s.at[j], vb_r.at[j], (w_at(j), z, f))

    def second_over(j):
        piece = w2_all.at[w_at(nw - j), :, f]
        if j:
            arrived(piece, vb_s.at[j], vb_r.at[j])
        send(piece, piece, vc_s.at[j], vc_r.at[j], partner)

    def whole(layer):
        dst = weights[layer]
        if not gather:
            own_w[layer].wait()
        elif layer == 0:
            for k in range(nz):
                arrived(dst.at[:, z_at(nz - k), other], fc_s.at[k], fc_r.at[k])
        else:
            for j in range(nw):
                arrived(dst.at[w_at(nw - j), :, other], vc_s.at[j], vc_r.at[j])
        return dst[...].reshape(width, width)

    def give(c):
        rows = pl.ds(other * own + c * CHUNK, CHUNK)
        send(
            tang_ref.at[rows], x.at[pl.ds(c * CHUNK, CHUNK), :, my_cols],
            ps.at[2 + c], pr.at[2 + c], partner,
        )

    if gather:
        along_z(0)
        pass_across(0)
    for i, src in enumerate((value_ref, lap_ref)):
        send(src.at[theirs, :], vl.at[i, :, my_cols], ps.at[i], pr.at[i], partner)
    give(0)
    if gather:
        along_z(1)
        for k in range(1, nz):
            from_z(0, k)
            pass_across(k)
            if k < chunks:
                give(k)
            pass_over(k - 1)
        pass_over(nz - 1)
        for c in range(nz, chunks):
            give(c)
        for k in range(1, nz):
            from_z(1, k)
        second_across()
        second_over(0)
    else:
        for c in range(1, chunks):
            give(c)

    for copy in own_vec + own_vl:
        copy.wait()
    for i in range(2):
        arrived(vl.at[i, :, their_cols], ps.at[i], pr.at[i])
    b1, b2, readout = vec[0], vec[1], vec[2]

    w1 = whole(0)
    vl_one = dot(vl[...].reshape(2 * own, width), w1)
    hidden_one = jnp.tanh(vl_one[:own] + b1)
    lapin_one = vl_one[own:]
    slope_one = 1.0 - hidden_one * hidden_one
    bend_one = -2.0 * hidden_one * slope_one
    slope_s[...] = slope_one

    def first(c, carry):
        own_part = x.at[pl.ds(c * CHUNK, CHUNK), :, my_cols]
        pltpu.make_async_copy(own_part, own_part, loc.at[tang_at + c]).wait()
        arrived(x.at[pl.ds(c * CHUNK, CHUNK), :, their_cols], ps.at[2 + c], pr.at[2 + c])
        block = x[pl.ds(c * CHUNK, CHUNK)].reshape(CHUNK * cols, width)
        grad = dot(block, w1)
        for i in range(CHUNK):
            row = c * CHUNK + i
            g = grad[i * cols:(i + 1) * cols]
            curv1_s[pl.ds(row, 1), :] = jnp.sum(g * g, axis=0, keepdims=True)
            x[row] = (slope_s[pl.ds(row, 1), :] * g).astype(BF16)
        return carry

    lax.fori_loop(0, chunks - 1, first, 0)
    if gather:
        for j in range(1, nw):
            second_over(j)
    first(chunks - 1, 0)

    w2 = whole(1)
    first_z = z == 0
    lap_two = bend_one * curv1_s[...] + jnp.where(first_z, slope_one * lapin_one, 0.0)
    vl_two = dot(jnp.concatenate([hidden_one.astype(BF16), halves(lap_two)], axis=0), w2)
    hidden_two = jnp.tanh(vl_two[:own] + b2)
    lapin_two = vl_two[own:2 * own] + vl_two[2 * own:]
    slope_two = 1.0 - hidden_two * hidden_two
    bend_two = -2.0 * hidden_two * slope_two
    weight_s[...] = readout * slope_two

    def second(c, carry):
        block = x[pl.ds(c * CHUNK, CHUNK)].reshape(CHUNK * cols, width)
        grad = dot(block, w2)
        for i in range(CHUNK):
            row = c * CHUNK + i
            g = grad[i * cols:(i + 1) * cols]
            curv2_s[pl.ds(row, 1), :] = jnp.sum(g * g, axis=0, keepdims=True)
            terms = weight_s[pl.ds(row, 1), :] * g
            terms = sum(terms[:, j:j + 128] for j in range(0, width, 128))
            gbuf[pl.ds(row, 1), :] = jnp.sum(terms.T, axis=0, keepdims=True)
        return carry

    lax.fori_loop(0, chunks, second, 0)

    send(gbuf, grad_out.at[mine, :], gs, gr, partner)
    keep = pltpu.make_async_copy(gbuf, grad_out.at[mine, :], loc.at[len(local)])
    keep.start()
    gradient = gbuf[...]
    part = jnp.sum(
        readout * (slope_two * lapin_two + bend_two * curv2_s[...]), axis=1, keepdims=True
    ) + jnp.sum(gradient * gradient, axis=1, keepdims=True)
    amp = jnp.where(first_z, jnp.sum(readout * hidden_two, axis=1, keepdims=True), 0.0)
    lane = lax.broadcasted_iota(jnp.int32, (own, 128), 1)
    place = lane == lax.broadcasted_iota(jnp.int32, (own, 128), 0) + f * own
    kin_row = jnp.sum(jnp.where(place, part, 0.0), axis=0, keepdims=True)
    amp_row = jnp.sum(jnp.where(place, amp, 0.0), axis=0, keepdims=True)
    tile_row = lax.broadcasted_iota(jnp.int32, (8, 128), 0)
    msg[z, f] = jnp.where(tile_row == 0, amp_row, -0.5 * kin_row)
    slot = msg.at[z, f]
    others = [(k, g) for k in range(nz) for g in range(2) if k or g]
    for k, g in others:
        send(slot, slot, ms.at[k, g], mr.at[k, g], (w, z_at(k), other if g else f))
    for k, g in others:
        arrived(msg.at[z_at(nz - k), other if g else f], ms.at[k, g], mr.at[k, g])
    total = msg[0, 0] + msg[0, 1]
    for k in range(1, nz):
        total = total + (msg[k, 0] + msg[k, 1])
    amp_out[...] = total[0:1, :2 * own]
    kin_out[...] = total[1:2, :2 * own]
    arrived(grad_out.at[theirs, :], gs, gr)
    keep.wait()
    for copy in sent:
        copy.wait_send()


def hand_over(*refs):
    sems = refs[-1]
    copies = [pltpu.make_async_copy(refs[i], refs[3 + i], sems.at[i]) for i in range(3)]
    for copy in copies:
        copy.start()
    for copy in copies:
        copy.wait()


def per_device(nw, nz, value_in, tang_in, lap_in, w_first, b_first, w_second, b_second, readout):
    walkers, cols, half = tang_in.shape
    width, own = 2 * half, walkers // 2
    shard = w_first.shape[0]
    gather = shard % 16 == 0
    if gather:
        w_shape = (nw, nz, 2, shard, width)
    else:
        w_shape = (width, width)
        w_first, w_second = (
            lax.all_gather(a, ("walker", "tangent", "feat"), axis=0, tiled=True) for a in (w_first, w_second)
        )
    chunks = own // CHUNK
    dma = pltpu.SemaphoreType.DMA
    in_hbm = pl.BlockSpec(memory_space=pltpu.HBM)
    in_vmem = pl.BlockSpec(memory_space=pltpu.VMEM)
    rows = own * cols
    row = jax.ShapeDtypeStruct((1, walkers), F32)
    results = pl.pallas_call(
        functools.partial(kernel, nw, nz, gather),
        out_shape=(jax.ShapeDtypeStruct((walkers, cols), F32), row, row),
        in_specs=[in_hbm] * 8,
        out_specs=(in_hbm, in_vmem, in_vmem),
        scratch_shapes=[
            pltpu.VMEM((own, cols, width), BF16),
            pltpu.VMEM(w_shape, BF16),
            pltpu.VMEM(w_shape, BF16),
            pltpu.VMEM((2, own, width), BF16),
            pltpu.VMEM((3, 1, width), F32),
            pltpu.VMEM((own, width), F32),
            pltpu.VMEM((own, width), F32),
            pltpu.VMEM((own, width), F32),
            pltpu.VMEM((own, width), F32),
            pltpu.VMEM((own, cols), F32),
            pltpu.VMEM((nz, 2, 8, 128), F32),
            dma((8 + chunks,)),
            dma((2 + chunks,)),
            dma((2 + chunks,)),
            dma((2, nz)),
            dma((2, nz)),
            dma((nz, nw)),
            dma((nz, nw)),
            dma((nz,)),
            dma((nz,)),
            dma((nw,)),
            dma((nw,)),
            dma((nw,)),
            dma((nw,)),
            dma,
            dma,
            dma((nz, 2)),
            dma((nz, 2)),
        ],
        compiler_params=pltpu.CompilerParams(
            collective_id=0, has_side_effects=True, vmem_limit_bytes=64 * 2**20
        ),
        cost_estimate=pl.CostEstimate(
            flops=4 * rows * width * width, bytes_accessed=2 * rows * width, transcendentals=0
        ),
    )(
        value_in, tang_in, lap_in, w_first, b_first.reshape(1, width),
        w_second, b_second.reshape(1, width), readout.reshape(1, width),
    )
    grad, amp, kin = pl.pallas_call(
        hand_over,
        out_shape=[jax.ShapeDtypeStruct(a.shape, a.dtype) for a in results],
        in_specs=[in_hbm] * 3,
        out_specs=[in_hbm] * 3,
        scratch_shapes=[dma((3,))],
    )(*results)
    return (amp.reshape(walkers), grad, kin.reshape(walkers))


def solution(mesh):
    placed = (
        P("walker", "feat"),
        P("walker", "tangent", "feat"),
        P("walker", "feat"),
        P(("walker", "tangent", "feat"), None),
        P(),
        P(("walker", "tangent", "feat"), None),
        P(),
        P(),
    )
    return jax.shard_map(
        functools.partial(per_device, mesh.shape["walker"], mesh.shape["tangent"]),
        mesh=mesh,
        in_specs=placed,
        out_specs=(P("walker"), P("walker", "tangent"), P("walker")),
        check_vma=False,
    )
```

```python
import functools

import jax
import jax.numpy as jnp
from jax import lax
from jax.experimental import pallas as pl
from jax.experimental.pallas import tpu as pltpu
from jax.sharding import PartitionSpec as P

F32 = jnp.float32
BF16 = jnp.bfloat16
MESH = pl.DeviceIdType.MESH
CHUNK = 4


def dot(a, b):
    return jnp.dot(a, b, preferred_element_type=F32)


def halves(a):
    high = a.astype(BF16)
    low = (a - high.astype(F32)).astype(BF16)
    return jnp.concatenate([high, low], axis=0)


def kernel(
    nw, nz, gather,
    value_ref, tang_ref, lap_ref, w1_ref, b1_ref, w2_ref, b2_ref, r_ref,
    grad_out, amp_out, kin_out,
    x, x_two, w1_all, w2_all, vl, vec, slope_s, weight_s, curv1_s, curv2_s, gbuf, msg,
    loc, ps, pr, za_s, za_r, wb_s, wb_r, fc_s, fc_r, vb_s, vb_r, vc_s, vc_r, gs, gr, ms, mr,
):
    w, z, f = lax.axis_index("walker"), lax.axis_index("tangent"), lax.axis_index("feat")
    other = 1 - f
    own, cols, width = x.shape
    half = width // 2
    parts = (slice(0, half), slice(half, width))
    chunks = own // CHUNK
    mine = pl.ds(pl.multiple_of(f * own, own), own)
    theirs = pl.ds(pl.multiple_of(other * own, own), own)
    my_cols = pl.ds(pl.multiple_of(f * half, half), half)
    their_cols = pl.ds(pl.multiple_of(other * half, half), half)
    partner = (w, z, other)

    def z_at(k):
        return lax.rem(z + k, nz)

    def w_at(k):
        return lax.rem(w + k, nw)

    def remote(src, dst, send, recv, device):
        return pltpu.make_async_remote_copy(
            src_ref=src, dst_ref=dst, send_sem=send, recv_sem=recv, device_id=device, device_id_type=MESH
        )

    local = []

    def fetch(src, dst):
        copy = pltpu.make_async_copy(src, dst, loc.at[len(local)])
        copy.start()
        local.append(copy)
        return copy

    own_w = [
        fetch(src, dst.at[w, z, f] if gather else dst) for src, dst in ((w1_ref, w1_all), (w2_ref, w2_all))
    ]
    own_vec = [fetch(src, vec.at[i]) for i, src in enumerate((b1_ref, b2_ref, r_ref))]
    own_vl = [fetch(src.at[mine, :], vl.at[i, :, my_cols]) for i, src in enumerate((value_ref, lap_ref))]
    tang_at = len(local)
    for c in range(chunks):
        rows = pl.ds(f * own + c * CHUNK, CHUNK)
        fetch(tang_ref.at[rows], x.at[pl.ds(c * CHUNK, CHUNK), :, my_cols])

    barrier = pltpu.get_barrier_semaphore()
    greeted = [partner]
    for k in range(1, nz):
        greeted += [(w, z_at(k), f), (w, z_at(k), other)]
    if gather:
        greeted += [(w_at(k), z, f) for k in range(1, nw)]
    for device in greeted:
        pl.semaphore_signal(barrier, inc=1, device_id=device, device_id_type=MESH)
    if gather:
        for copy in own_w:
            copy.wait()
    pl.semaphore_wait(barrier, len(greeted))

    sent = []

    def send(*args):
        copy = remote(*args)
        copy.start()
        sent.append(copy)

    def arrived(ref, send_sem, recv_sem):
        remote(ref, ref, send_sem, recv_sem, partner).wait_recv()

    weights = (w1_all, w2_all)

    def along_z(layer):
        piece = weights[layer].at[w, z, f]
        for k in range(1, nz):
            send(piece, piece, za_s.at[layer, k], za_r.at[layer, k], (w, z_at(k), f))

    def from_z(layer, k):
        arrived(weights[layer].at[w, z_at(nz - k), f], za_s.at[layer, k], za_r.at[layer, k])

    def pass_across(k):
        piece = w1_all.at[w, z_at(nz - k), f]
        for j in range(1, nw):
            send(piece, piece, wb_s.at[k, j], wb_r.at[k, j], (w_at(j), z, f))

    def pass_over(k):
        for j in range(1, nw):
            arrived(w1_all.at[w_at(nw - j), z_at(nz - k), f], wb_s.at[k, j], wb_r.at[k, j])
        piece = w1_all.at[:, z_at(nz - k), f]
        send(piece, piece, fc_s.at[k], fc_r.at[k], partner)

    def second_across():
        piece = w2_all.at[w, :, f]
        for j in range(1, nw):
            send(piece, piece, vb_s.at[j], vb_r.at[j], (w_at(j), z, f))

    def second_over(j):
        piece = w2_all.at[w_at(nw - j), :, f]
        if j:
            arrived(piece, vb_s.at[j], vb_r.at[j])
        send(piece, piece, vc_s.at[j], vc_r.at[j], partner)

    def whole(layer):
        dst = weights[layer]
        if not gather:
            own_w[layer].wait()
        elif layer == 0:
            for k in range(nz):
                arrived(dst.at[:, z_at(nz - k), other], fc_s.at[k], fc_r.at[k])
        else:
            for j in range(nw):
                arrived(dst.at[w_at(nw - j), :, other], vc_s.at[j], vc_r.at[j])
        return dst[...].reshape(width, width)

    def give(c):
        rows = pl.ds(other * own + c * CHUNK, CHUNK)
        send(
            tang_ref.at[rows], x.at[pl.ds(c * CHUNK, CHUNK), :, my_cols],
            ps.at[2 + c], pr.at[2 + c], partner,
        )

    if gather:
        along_z(0)
        pass_across(0)
    for i, src in enumerate((value_ref, lap_ref)):
        send(src.at[theirs, :], vl.at[i, :, my_cols], ps.at[i], pr.at[i], partner)
    give(0)
    if gather:
        along_z(1)
        for k in range(1, nz):
            from_z(0, k)
            pass_across(k)
            if k < chunks:
                give(k)
            pass_over(k - 1)
        for c in range(nz, chunks):
            give(c)
        for k in range(1, nz):
            from_z(1, k)
        second_across()
        pass_over(nz - 1)
        second_over(0)
    else:
        for c in range(1, chunks):
            give(c)

    for copy in own_vec + own_vl:
        copy.wait()
    for i in range(2):
        arrived(vl.at[i, :, their_cols], ps.at[i], pr.at[i])
    b1, b2, readout = vec[0], vec[1], vec[2]

    w1 = whole(0)
    vl_one = dot(vl[...].reshape(2 * own, width), w1)
    hidden_one = jnp.tanh(vl_one[:own] + b1)
    lapin_one = vl_one[own:]
    slope_one = 1.0 - hidden_one * hidden_one
    bend_one = -2.0 * hidden_one * slope_one
    slope_s[...] = slope_one

    def first(c, carry):
        own_part = x.at[pl.ds(c * CHUNK, CHUNK), :, my_cols]
        pltpu.make_async_copy(own_part, own_part, loc.at[tang_at + c]).wait()
        arrived(x.at[pl.ds(c * CHUNK, CHUNK), :, their_cols], ps.at[2 + c], pr.at[2 + c])
        block = x[pl.ds(c * CHUNK, CHUNK)].reshape(CHUNK * cols, width)
        for part in parts:
            grad = dot(block, w1[:, part])
            for i in range(CHUNK):
                row = c * CHUNK + i
                g = grad[i * cols:(i + 1) * cols]
                curv1_s[pl.ds(row, 1), part] = jnp.sum(g * g, axis=0, keepdims=True)
                x_two[row, :, part] = (slope_s[pl.ds(row, 1), part] * g).astype(BF16)
        return carry

    lax.fori_loop(0, chunks - 1, first, 0)
    if gather:
        for j in range(1, nw):
            second_over(j)
    first(chunks - 1, 0)

    w2 = whole(1)
    first_z = z == 0
    lap_two = bend_one * curv1_s[...] + jnp.where(first_z, slope_one * lapin_one, 0.0)
    vl_two = dot(jnp.concatenate([hidden_one.astype(BF16), halves(lap_two)], axis=0), w2)
    hidden_two = jnp.tanh(vl_two[:own] + b2)
    lapin_two = vl_two[own:2 * own] + vl_two[2 * own:]
    slope_two = 1.0 - hidden_two * hidden_two
    bend_two = -2.0 * hidden_two * slope_two
    weight_s[...] = readout * slope_two

    def second(c, carry):
        block = x_two[pl.ds(c * CHUNK, CHUNK)].reshape(CHUNK * cols, width)
        folded = [0.0] * CHUNK
        for part in parts:
            grad = dot(block, w2[:, part])
            for i in range(CHUNK):
                row = c * CHUNK + i
                g = grad[i * cols:(i + 1) * cols]
                curv2_s[pl.ds(row, 1), part] = jnp.sum(g * g, axis=0, keepdims=True)
                terms = weight_s[pl.ds(row, 1), part] * g
                folded[i] += sum(terms[:, j:j + 128] for j in range(0, terms.shape[1], 128))
        for i in range(CHUNK):
            gbuf[pl.ds(c * CHUNK + i, 1), :] = jnp.sum(folded[i].T, axis=0, keepdims=True)
        return carry

    lax.fori_loop(0, chunks, second, 0)

    send(gbuf, grad_out.at[mine, :], gs, gr, partner)
    keep = pltpu.make_async_copy(gbuf, grad_out.at[mine, :], loc.at[len(local)])
    keep.start()
    gradient = gbuf[...]
    part = jnp.sum(
        readout * (slope_two * lapin_two + bend_two * curv2_s[...]), axis=1, keepdims=True
    ) + jnp.sum(gradient * gradient, axis=1, keepdims=True)
    amp = jnp.where(first_z, jnp.sum(readout * hidden_two, axis=1, keepdims=True), 0.0)
    lane = lax.broadcasted_iota(jnp.int32, (own, 128), 1)
    place = lane == lax.broadcasted_iota(jnp.int32, (own, 128), 0) + f * own
    kin_row = jnp.sum(jnp.where(place, part, 0.0), axis=0, keepdims=True)
    amp_row = jnp.sum(jnp.where(place, amp, 0.0), axis=0, keepdims=True)
    tile_row = lax.broadcasted_iota(jnp.int32, (8, 128), 0)
    msg[z, f] = jnp.where(tile_row == 0, amp_row, -0.5 * kin_row)
    slot = msg.at[z, f]
    others = [(k, g) for k in range(nz) for g in range(2) if k or g]
    for k, g in others:
        send(slot, slot, ms.at[k, g], mr.at[k, g], (w, z_at(k), other if g else f))
    for k, g in others:
        arrived(msg.at[z_at(nz - k), other if g else f], ms.at[k, g], mr.at[k, g])
    total = msg[0, 0] + msg[0, 1]
    for k in range(1, nz):
        total = total + (msg[k, 0] + msg[k, 1])
    amp_out[...] = total[0:1, :2 * own]
    kin_out[...] = total[1:2, :2 * own]
    arrived(grad_out.at[theirs, :], gs, gr)
    keep.wait()
    for copy in sent:
        copy.wait_send()


def hand_over(*refs):
    sems = refs[-1]
    reads = [pltpu.make_async_copy(refs[i], refs[6 + i], sems.at[i]) for i in range(3)]
    writes = [pltpu.make_async_copy(refs[6 + i], refs[3 + i], sems.at[3 + i]) for i in range(3)]
    for copy in reads:
        copy.start()
    for read, write in zip(reads, writes):
        read.wait()
        write.start()
    for copy in writes:
        copy.wait()


def per_device(nw, nz, value_in, tang_in, lap_in, w_first, b_first, w_second, b_second, readout):
    walkers, cols, half = tang_in.shape
    width, own = 2 * half, walkers // 2
    shard = w_first.shape[0]
    gather = shard % 16 == 0
    if gather:
        w_shape = (nw, nz, 2, shard, width)
    else:
        w_shape = (width, width)
        w_first, w_second = (
            lax.all_gather(a, ("walker", "tangent", "feat"), axis=0, tiled=True) for a in (w_first, w_second)
        )
    chunks = own // CHUNK
    dma = pltpu.SemaphoreType.DMA
    in_hbm = pl.BlockSpec(memory_space=pltpu.HBM)
    in_vmem = pl.BlockSpec(memory_space=pltpu.VMEM)
    rows = own * cols
    row = jax.ShapeDtypeStruct((1, walkers), F32)
    results = pl.pallas_call(
        functools.partial(kernel, nw, nz, gather),
        out_shape=(jax.ShapeDtypeStruct((walkers, cols), F32), row, row),
        in_specs=[in_hbm] * 8,
        out_specs=(in_hbm, in_vmem, in_vmem),
        scratch_shapes=[
            pltpu.VMEM((own, cols, width), BF16),
            pltpu.VMEM((own, cols, width), BF16),
            pltpu.VMEM(w_shape, BF16),
            pltpu.VMEM(w_shape, BF16),
            pltpu.VMEM((2, own, width), BF16),
            pltpu.VMEM((3, 1, width), F32),
            pltpu.VMEM((own, width), F32),
            pltpu.VMEM((own, width), F32),
            pltpu.VMEM((own, width), F32),
            pltpu.VMEM((own, width), F32),
            pltpu.VMEM((own, cols), F32),
            pltpu.VMEM((nz, 2, 8, 128), F32),
            dma((8 + chunks,)),
            dma((2 + chunks,)),
            dma((2 + chunks,)),
            dma((2, nz)),
            dma((2, nz)),
            dma((nz, nw)),
            dma((nz, nw)),
            dma((nz,)),
            dma((nz,)),
            dma((nw,)),
            dma((nw,)),
            dma((nw,)),
            dma((nw,)),
            dma,
            dma,
            dma((nz, 2)),
            dma((nz, 2)),
        ],
        compiler_params=pltpu.CompilerParams(
            collective_id=0, has_side_effects=True, vmem_limit_bytes=64 * 2**20
        ),
        cost_estimate=pl.CostEstimate(
            flops=4 * rows * width * width, bytes_accessed=2 * rows * width, transcendentals=0
        ),
    )(
        value_in, tang_in, lap_in, w_first, b_first.reshape(1, width),
        w_second, b_second.reshape(1, width), readout.reshape(1, width),
    )
    grad, amp, kin = pl.pallas_call(
        hand_over,
        out_shape=[jax.ShapeDtypeStruct(a.shape, a.dtype) for a in results],
        in_specs=[in_hbm] * 3,
        out_specs=[in_hbm] * 3,
        scratch_shapes=[pltpu.VMEM(a.shape, a.dtype) for a in results] + [dma((6,))],
        compiler_params=pltpu.CompilerParams(vmem_limit_bytes=64 * 2**20),
    )(*results)
    return (amp.reshape(walkers), grad, kin.reshape(walkers))


def solution(mesh):
    placed = (
        P("walker", "feat"),
        P("walker", "tangent", "feat"),
        P("walker", "feat"),
        P(("walker", "tangent", "feat"), None),
        P(),
        P(("walker", "tangent", "feat"), None),
        P(),
        P(),
    )
    return jax.shard_map(
        functools.partial(per_device, mesh.shape["walker"], mesh.shape["tangent"]),
        mesh=mesh,
        in_specs=placed,
        out_specs=(P("walker"), P("walker", "tangent"), P("walker")),
        check_vma=False,
    )
```

```python
import functools

import jax
import jax.numpy as jnp
from jax import lax
from jax.experimental import pallas as pl
from jax.experimental.pallas import tpu as pltpu
from jax.sharding import PartitionSpec as P

F32 = jnp.float32
BF16 = jnp.bfloat16
MESH = pl.DeviceIdType.MESH
CHUNK = 4


def dot(a, b):
    return jnp.dot(a, b, preferred_element_type=F32)


def halves(a):
    high = a.astype(BF16)
    low = (a - high.astype(F32)).astype(BF16)
    return jnp.concatenate([high, low], axis=0)


def kernel(
    nw, nz, gather,
    value_ref, tang_ref, lap_ref, w1_ref, b1_ref, w2_ref, b2_ref, r_ref,
    grad_out, amp_out, kin_out,
    x, x_two, w1_all, w2_all, vl, vec, slope_s, weight_s, curv1_s, curv2_s, gbuf, msg,
    loc, ps, pr, za_s, za_r, wb_s, wb_r, wx_s, wx_r, fc_s, fc_r, vb_s, vb_r, vc_s, vc_r, gs, gr, ms, mr,
):
    w, z, f = lax.axis_index("walker"), lax.axis_index("tangent"), lax.axis_index("feat")
    other = 1 - f
    own, cols, width = x.shape
    half = width // 2
    parts = (slice(0, half), slice(half, width))
    chunks = own // CHUNK
    mine = pl.ds(pl.multiple_of(f * own, own), own)
    theirs = pl.ds(pl.multiple_of(other * own, own), own)
    my_cols = pl.ds(pl.multiple_of(f * half, half), half)
    their_cols = pl.ds(pl.multiple_of(other * half, half), half)
    partner = (w, z, other)

    def flipped(index, k):
        bit = 1
        while bit <= k:
            if (k // bit) % 2:
                index = index + bit - 2 * bit * lax.rem(lax.div(index, bit), 2)
            bit *= 2
        return index

    def z_at(k):
        return flipped(z, k)

    def w_at(k):
        return flipped(w, k)

    def remote(src, dst, send, recv, device):
        return pltpu.make_async_remote_copy(
            src_ref=src, dst_ref=dst, send_sem=send, recv_sem=recv, device_id=device, device_id_type=MESH
        )

    local = []

    def fetch(src, dst):
        copy = pltpu.make_async_copy(src, dst, loc.at[len(local)])
        copy.start()
        local.append(copy)
        return copy

    own_w = [
        fetch(src, dst.at[w, z, f] if gather else dst) for src, dst in ((w1_ref, w1_all), (w2_ref, w2_all))
    ]
    own_vec = [fetch(src, vec.at[i]) for i, src in enumerate((b1_ref, b2_ref, r_ref))]
    own_vl = [fetch(src.at[mine, :], vl.at[i, :, my_cols]) for i, src in enumerate((value_ref, lap_ref))]
    tang_at = len(local)
    for c in range(chunks):
        rows = pl.ds(f * own + c * CHUNK, CHUNK)
        fetch(tang_ref.at[rows], x.at[pl.ds(c * CHUNK, CHUNK), :, my_cols])

    barrier = pltpu.get_barrier_semaphore()
    greeted = [partner]
    for k in range(1, nz):
        greeted += [(w, z_at(k), f), (w, z_at(k), other)]
    if gather:
        for k in range(1, nw):
            greeted += [(w_at(k), z, f), (w_at(k), z, other)]
    for device in greeted:
        pl.semaphore_signal(barrier, inc=1, device_id=device, device_id_type=MESH)
    if gather:
        for copy in own_w:
            copy.wait()
    pl.semaphore_wait(barrier, len(greeted))

    sent = []

    def send(*args):
        copy = remote(*args)
        copy.start()
        sent.append(copy)

    def arrived(ref, send_sem, recv_sem):
        remote(ref, ref, send_sem, recv_sem, partner).wait_recv()

    weights = (w1_all, w2_all)

    def along_z(layer):
        piece = weights[layer].at[w, z, f]
        for k in range(1, nz):
            send(piece, piece, za_s.at[layer, k], za_r.at[layer, k], (w, z_at(k), f))

    def from_z(layer, k):
        arrived(weights[layer].at[w, z_at(k), f], za_s.at[layer, k], za_r.at[layer, k])

    def pass_across(k):
        piece = w1_all.at[w, z_at(k), f]
        for j in range(1, nw):
            send(piece, piece, wb_s.at[k, j], wb_r.at[k, j], (w_at(j), z, f))
        if k == nz - 1:
            for j in range(nw):
                send(piece, piece, wx_s.at[j], wx_r.at[j], (w_at(j), z, other))

    def pass_over(k):
        for j in range(1, nw):
            arrived(w1_all.at[w_at(j), z_at(k), f], wb_s.at[k, j], wb_r.at[k, j])
        if k < nz - 1:
            piece = w1_all.at[:, z_at(k), f]
            send(piece, piece, fc_s.at[k], fc_r.at[k], partner)

    def second_across():
        piece = w2_all.at[w, :, f]
        for j in range(1, nw):
            send(piece, piece, vb_s.at[j], vb_r.at[j], (w_at(j), z, f))

    def second_over(j):
        piece = w2_all.at[w_at(j), :, f]
        if j:
            arrived(piece, vb_s.at[j], vb_r.at[j])
        send(piece, piece, vc_s.at[j], vc_r.at[j], partner)

    def whole(layer):
        dst = weights[layer]
        if not gather:
            own_w[layer].wait()
        elif layer == 0:
            for k in range(nz - 1):
                arrived(dst.at[:, z_at(k), other], fc_s.at[k], fc_r.at[k])
            for j in range(nw):
                arrived(dst.at[w_at(j), z_at(nz - 1), other], wx_s.at[j], wx_r.at[j])
        else:
            for j in range(nw):
                arrived(dst.at[w_at(j), :, other], vc_s.at[j], vc_r.at[j])
        return dst[...].reshape(width, width)

    def give(c):
        rows = pl.ds(other * own + c * CHUNK, CHUNK)
        send(
            tang_ref.at[rows], x.at[pl.ds(c * CHUNK, CHUNK), :, my_cols],
            ps.at[2 + c], pr.at[2 + c], partner,
        )

    if gather:
        along_z(0)
        pass_across(0)
    for i, src in enumerate((value_ref, lap_ref)):
        send(src.at[theirs, :], vl.at[i, :, my_cols], ps.at[i], pr.at[i], partner)
    give(0)
    if gather:
        along_z(1)
        for k in range(1, nz):
            from_z(0, k)
            pass_across(k)
            if k < chunks:
                give(k)
            pass_over(k - 1)
        for c in range(nz, chunks):
            give(c)
        for k in range(1, nz):
            from_z(1, k)
        second_across()
        pass_over(nz - 1)
        second_over(0)
    else:
        for c in range(1, chunks):
            give(c)

    for copy in own_vec + own_vl:
        copy.wait()
    for i in range(2):
        arrived(vl.at[i, :, their_cols], ps.at[i], pr.at[i])
    b1, b2, readout = vec[0], vec[1], vec[2]

    w1 = whole(0)
    vl_one = dot(vl[...].reshape(2 * own, width), w1)
    hidden_one = jnp.tanh(vl_one[:own] + b1)
    lapin_one = vl_one[own:]
    slope_one = 1.0 - hidden_one * hidden_one
    bend_one = -2.0 * hidden_one * slope_one
    slope_s[...] = slope_one

    def first(c, carry):
        own_part = x.at[pl.ds(c * CHUNK, CHUNK), :, my_cols]
        pltpu.make_async_copy(own_part, own_part, loc.at[tang_at + c]).wait()
        arrived(x.at[pl.ds(c * CHUNK, CHUNK), :, their_cols], ps.at[2 + c], pr.at[2 + c])
        block = x[pl.ds(c * CHUNK, CHUNK)].reshape(CHUNK * cols, width)
        for part in parts:
            grad = dot(block, w1[:, part])
            for i in range(CHUNK):
                row = c * CHUNK + i
                g = grad[i * cols:(i + 1) * cols]
                curv1_s[pl.ds(row, 1), part] = jnp.sum(g * g, axis=0, keepdims=True)
                x_two[row, :, part] = (slope_s[pl.ds(row, 1), part] * g).astype(BF16)
        return carry

    lax.fori_loop(0, chunks - 1, first, 0)
    if gather:
        for j in range(1, nw):
            second_over(j)
    first(chunks - 1, 0)

    w2 = whole(1)
    first_z = z == 0
    lap_two = bend_one * curv1_s[...] + jnp.where(first_z, slope_one * lapin_one, 0.0)
    vl_two = dot(jnp.concatenate([hidden_one.astype(BF16), halves(lap_two)], axis=0), w2)
    hidden_two = jnp.tanh(vl_two[:own] + b2)
    lapin_two = vl_two[own:2 * own] + vl_two[2 * own:]
    slope_two = 1.0 - hidden_two * hidden_two
    bend_two = -2.0 * hidden_two * slope_two
    weight_s[...] = readout * slope_two

    def second(c, carry):
        block = x_two[pl.ds(c * CHUNK, CHUNK)].reshape(CHUNK * cols, width)
        folded = [0.0] * CHUNK
        for part in parts:
            grad = dot(block, w2[:, part])
            for i in range(CHUNK):
                row = c * CHUNK + i
                g = grad[i * cols:(i + 1) * cols]
                curv2_s[pl.ds(row, 1), part] = jnp.sum(g * g, axis=0, keepdims=True)
                terms = weight_s[pl.ds(row, 1), part] * g
                folded[i] += sum(terms[:, j:j + 128] for j in range(0, terms.shape[1], 128))
        for i in range(CHUNK):
            gbuf[pl.ds(c * CHUNK + i, 1), :] = jnp.sum(folded[i].T, axis=0, keepdims=True)
        return carry

    lax.fori_loop(0, chunks, second, 0)

    send(gbuf, grad_out.at[mine, :], gs, gr, partner)
    keep = pltpu.make_async_copy(gbuf, grad_out.at[mine, :], loc.at[len(local)])
    keep.start()
    gradient = gbuf[...]
    part = jnp.sum(
        readout * (slope_two * lapin_two + bend_two * curv2_s[...]), axis=1, keepdims=True
    ) + jnp.sum(gradient * gradient, axis=1, keepdims=True)
    amp = jnp.where(first_z, jnp.sum(readout * hidden_two, axis=1, keepdims=True), 0.0)
    lane = lax.broadcasted_iota(jnp.int32, (own, 128), 1)
    place = lane == lax.broadcasted_iota(jnp.int32, (own, 128), 0) + f * own
    kin_row = jnp.sum(jnp.where(place, part, 0.0), axis=0, keepdims=True)
    amp_row = jnp.sum(jnp.where(place, amp, 0.0), axis=0, keepdims=True)
    tile_row = lax.broadcasted_iota(jnp.int32, (8, 128), 0)
    msg[z, f] = jnp.where(tile_row == 0, amp_row, -0.5 * kin_row)
    slot = msg.at[z, f]
    others = [(k, g) for k in range(nz) for g in range(2) if k or g]
    for k, g in others:
        send(slot, slot, ms.at[k, g], mr.at[k, g], (w, z_at(k), other if g else f))
    for k, g in others:
        arrived(msg.at[z_at(k), other if g else f], ms.at[k, g], mr.at[k, g])
    total = msg[0, 0] + msg[0, 1]
    for k in range(1, nz):
        total = total + (msg[k, 0] + msg[k, 1])
    amp_out[...] = total[0:1, :2 * own]
    kin_out[...] = total[1:2, :2 * own]
    arrived(grad_out.at[theirs, :], gs, gr)
    keep.wait()
    for copy in sent:
        copy.wait_send()


def hand_over(*refs):
    sems = refs[-1]
    reads = [pltpu.make_async_copy(refs[i], refs[6 + i], sems.at[i]) for i in range(3)]
    writes = [pltpu.make_async_copy(refs[6 + i], refs[3 + i], sems.at[3 + i]) for i in range(3)]
    for copy in reads:
        copy.start()
    for read, write in zip(reads, writes):
        read.wait()
        write.start()
    for copy in writes:
        copy.wait()


def per_device(nw, nz, value_in, tang_in, lap_in, w_first, b_first, w_second, b_second, readout):
    walkers, cols, half = tang_in.shape
    width, own = 2 * half, walkers // 2
    shard = w_first.shape[0]
    gather = shard % 16 == 0
    if gather:
        w_shape = (nw, nz, 2, shard, width)
    else:
        w_shape = (width, width)
        w_first, w_second = (
            lax.all_gather(a, ("walker", "tangent", "feat"), axis=0, tiled=True) for a in (w_first, w_second)
        )
    chunks = own // CHUNK
    dma = pltpu.SemaphoreType.DMA
    in_hbm = pl.BlockSpec(memory_space=pltpu.HBM)
    in_vmem = pl.BlockSpec(memory_space=pltpu.VMEM)
    rows = own * cols
    row = jax.ShapeDtypeStruct((1, walkers), F32)
    results = pl.pallas_call(
        functools.partial(kernel, nw, nz, gather),
        out_shape=(jax.ShapeDtypeStruct((walkers, cols), F32), row, row),
        in_specs=[in_hbm] * 8,
        out_specs=(in_hbm, in_vmem, in_vmem),
        scratch_shapes=[
            pltpu.VMEM((own, cols, width), BF16),
            pltpu.VMEM((own, cols, width), BF16),
            pltpu.VMEM(w_shape, BF16),
            pltpu.VMEM(w_shape, BF16),
            pltpu.VMEM((2, own, width), BF16),
            pltpu.VMEM((3, 1, width), F32),
            pltpu.VMEM((own, width), F32),
            pltpu.VMEM((own, width), F32),
            pltpu.VMEM((own, width), F32),
            pltpu.VMEM((own, width), F32),
            pltpu.VMEM((own, cols), F32),
            pltpu.VMEM((nz, 2, 8, 128), F32),
            dma((8 + chunks,)),
            dma((2 + chunks,)),
            dma((2 + chunks,)),
            dma((2, nz)),
            dma((2, nz)),
            dma((nz, nw)),
            dma((nz, nw)),
            dma((nw,)),
            dma((nw,)),
            dma((nz,)),
            dma((nz,)),
            dma((nw,)),
            dma((nw,)),
            dma((nw,)),
            dma((nw,)),
            dma,
            dma,
            dma((nz, 2)),
            dma((nz, 2)),
        ],
        compiler_params=pltpu.CompilerParams(
            collective_id=0, has_side_effects=True, vmem_limit_bytes=64 * 2**20
        ),
        cost_estimate=pl.CostEstimate(
            flops=4 * rows * width * width, bytes_accessed=2 * rows * width, transcendentals=0
        ),
    )(
        value_in, tang_in, lap_in, w_first, b_first.reshape(1, width),
        w_second, b_second.reshape(1, width), readout.reshape(1, width),
    )
    grad, amp, kin = pl.pallas_call(
        hand_over,
        out_shape=[jax.ShapeDtypeStruct(a.shape, a.dtype) for a in results],
        in_specs=[in_hbm] * 3,
        out_specs=[in_hbm] * 3,
        scratch_shapes=[pltpu.VMEM(a.shape, a.dtype) for a in results] + [dma((6,))],
        compiler_params=pltpu.CompilerParams(vmem_limit_bytes=64 * 2**20),
    )(*results)
    return (amp.reshape(walkers), grad, kin.reshape(walkers))


def solution(mesh):
    placed = (
        P("walker", "feat"),
        P("walker", "tangent", "feat"),
        P("walker", "feat"),
        P(("walker", "tangent", "feat"), None),
        P(),
        P(("walker", "tangent", "feat"), None),
        P(),
        P(),
    )
    return jax.shard_map(
        functools.partial(per_device, mesh.shape["walker"], mesh.shape["tangent"]),
        mesh=mesh,
        in_specs=placed,
        out_specs=(P("walker"), P("walker", "tangent"), P("walker")),
        check_vma=False,
    )
```

```python
import functools

import jax
import jax.numpy as jnp
from jax import lax
from jax.experimental import pallas as pl
from jax.experimental.pallas import tpu as pltpu
from jax.sharding import PartitionSpec as P

F32 = jnp.float32
BF16 = jnp.bfloat16
MESH = pl.DeviceIdType.MESH
CHUNK = 4


def dot(a, b):
    return jnp.dot(a, b, preferred_element_type=F32)


def halves(a):
    high = a.astype(BF16)
    low = (a - high.astype(F32)).astype(BF16)
    return jnp.concatenate([high, low], axis=0)


def kernel(
    nw, nz, gather,
    value_ref, tang_ref, lap_ref, w1_ref, b1_ref, w2_ref, b2_ref, r_ref,
    grad_out, amp_out, kin_out,
    x, x_two, w1_all, w2_all, vl, vec, slope_s, weight_s, curv1_s, curv2_s, gbuf, msg,
    loc, ps, pr, za_s, za_r, wb_s, wb_r, wx_s, wx_r, fc_s, fc_r, vb_s, vb_r, vc_s, vc_r, gs, gr, ms, mr,
):
    w, z, f = lax.axis_index("walker"), lax.axis_index("tangent"), lax.axis_index("feat")
    other = 1 - f
    own, cols, width = x.shape
    half = width // 2
    parts = (slice(0, half), slice(half, width))
    chunks = own // CHUNK
    mine = pl.ds(pl.multiple_of(f * own, own), own)
    theirs = pl.ds(pl.multiple_of(other * own, own), own)
    my_cols = pl.ds(pl.multiple_of(f * half, half), half)
    their_cols = pl.ds(pl.multiple_of(other * half, half), half)
    partner = (w, z, other)

    def flipped(index, k):
        bit = 1
        while bit <= k:
            if (k // bit) % 2:
                index = index + bit - 2 * bit * lax.rem(lax.div(index, bit), 2)
            bit *= 2
        return index

    def z_at(k):
        return flipped(z, k)

    def w_at(k):
        return flipped(w, k)

    def remote(src, dst, send, recv, device):
        return pltpu.make_async_remote_copy(
            src_ref=src, dst_ref=dst, send_sem=send, recv_sem=recv, device_id=device, device_id_type=MESH
        )

    local = []

    def fetch(src, dst):
        copy = pltpu.make_async_copy(src, dst, loc.at[len(local)])
        copy.start()
        local.append(copy)
        return copy

    own_w = [
        fetch(src, dst.at[w, z, f] if gather else dst) for src, dst in ((w1_ref, w1_all), (w2_ref, w2_all))
    ]
    own_vec = [fetch(src, vec.at[i]) for i, src in enumerate((b1_ref, b2_ref, r_ref))]
    own_vl = [fetch(src.at[mine, :], vl.at[i, :, my_cols]) for i, src in enumerate((value_ref, lap_ref))]
    tang_at = len(local)
    for c in range(chunks):
        rows = pl.ds(f * own + c * CHUNK, CHUNK)
        fetch(tang_ref.at[rows], x.at[pl.ds(c * CHUNK, CHUNK), :, my_cols])

    barrier = pltpu.get_barrier_semaphore()
    greeted = [partner]
    for k in range(1, nz):
        greeted += [(w, z_at(k), f), (w, z_at(k), other)]
    if gather:
        for k in range(1, nw):
            greeted += [(w_at(k), z, f), (w_at(k), z, other)]
    for device in greeted:
        pl.semaphore_signal(barrier, inc=1, device_id=device, device_id_type=MESH)
    if gather:
        for copy in own_w:
            copy.wait()
    pl.semaphore_wait(barrier, len(greeted))

    sent = []

    def send(*args):
        copy = remote(*args)
        copy.start()
        sent.append(copy)

    def arrived(ref, send_sem, recv_sem):
        remote(ref, ref, send_sem, recv_sem, partner).wait_recv()

    weights = (w1_all, w2_all)

    def along_z(layer):
        piece = weights[layer].at[w, z, f]
        for k in range(1, nz):
            send(piece, piece, za_s.at[layer, k], za_r.at[layer, k], (w, z_at(k), f))

    def from_z(layer, k):
        arrived(weights[layer].at[w, z_at(k), f], za_s.at[layer, k], za_r.at[layer, k])

    def pass_across(k):
        piece = w1_all.at[w, z_at(k), f]
        for j in range(1, nw):
            send(piece, piece, wb_s.at[k, j], wb_r.at[k, j], (w_at(j), z, f))
        if k == nz - 1:
            for j in range(nw):
                send(piece, piece, wx_s.at[j], wx_r.at[j], (w_at(j), z, other))

    def pass_over(k):
        for j in range(1, nw):
            arrived(w1_all.at[w_at(j), z_at(k), f], wb_s.at[k, j], wb_r.at[k, j])
        if k < nz - 1:
            piece = w1_all.at[:, z_at(k), f]
            send(piece, piece, fc_s.at[k], fc_r.at[k], partner)

    def second_across():
        piece = w2_all.at[w, :, f]
        for j in range(1, nw):
            send(piece, piece, vb_s.at[j], vb_r.at[j], (w_at(j), z, f))

    def second_over(j):
        piece = w2_all.at[w_at(j), :, f]
        if j:
            arrived(piece, vb_s.at[j], vb_r.at[j])
        send(piece, piece, vc_s.at[j], vc_r.at[j], partner)

    def whole(layer):
        dst = weights[layer]
        if not gather:
            own_w[layer].wait()
        elif layer == 0:
            for k in range(nz - 1):
                arrived(dst.at[:, z_at(k), other], fc_s.at[k], fc_r.at[k])
            for j in range(nw):
                arrived(dst.at[w_at(j), z_at(nz - 1), other], wx_s.at[j], wx_r.at[j])
        else:
            for j in range(nw):
                arrived(dst.at[w_at(j), :, other], vc_s.at[j], vc_r.at[j])
        return dst[...].reshape(width, width)

    def give(c):
        rows = pl.ds(other * own + c * CHUNK, CHUNK)
        send(
            tang_ref.at[rows], x.at[pl.ds(c * CHUNK, CHUNK), :, my_cols],
            ps.at[2 + c], pr.at[2 + c], partner,
        )

    if gather:
        along_z(0)
        pass_across(0)
    for i, src in enumerate((value_ref, lap_ref)):
        send(src.at[theirs, :], vl.at[i, :, my_cols], ps.at[i], pr.at[i], partner)
    if gather:
        along_z(1)
    for c in range(chunks):
        give(c)
    if gather:
        for k in range(1, nz):
            from_z(0, k)
            pass_across(k)
            pass_over(k - 1)
        for k in range(1, nz):
            from_z(1, k)
        second_across()
        pass_over(nz - 1)
        second_over(0)

    for copy in own_vec + own_vl:
        copy.wait()
    for i in range(2):
        arrived(vl.at[i, :, their_cols], ps.at[i], pr.at[i])
    b1, b2, readout = vec[0], vec[1], vec[2]

    w1 = whole(0)
    vl_one = dot(vl[...].reshape(2 * own, width), w1)
    hidden_one = jnp.tanh(vl_one[:own] + b1)
    lapin_one = vl_one[own:]
    slope_one = 1.0 - hidden_one * hidden_one
    bend_one = -2.0 * hidden_one * slope_one
    slope_s[...] = slope_one

    def first(c, carry):
        own_part = x.at[pl.ds(c * CHUNK, CHUNK), :, my_cols]
        pltpu.make_async_copy(own_part, own_part, loc.at[tang_at + c]).wait()
        arrived(x.at[pl.ds(c * CHUNK, CHUNK), :, their_cols], ps.at[2 + c], pr.at[2 + c])
        block = x[pl.ds(c * CHUNK, CHUNK)].reshape(CHUNK * cols, width)
        for part in parts:
            grad = dot(block, w1[:, part])
            for i in range(CHUNK):
                row = c * CHUNK + i
                g = grad[i * cols:(i + 1) * cols]
                curv1_s[pl.ds(row, 1), part] = jnp.sum(g * g, axis=0, keepdims=True)
                x_two[row, :, part] = (slope_s[pl.ds(row, 1), part] * g).astype(BF16)
        return carry

    lax.fori_loop(0, chunks - 1, first, 0)
    if gather:
        for j in range(1, nw):
            second_over(j)
    first(chunks - 1, 0)

    w2 = whole(1)
    first_z = z == 0
    lap_two = bend_one * curv1_s[...] + jnp.where(first_z, slope_one * lapin_one, 0.0)
    vl_two = dot(jnp.concatenate([hidden_one.astype(BF16), halves(lap_two)], axis=0), w2)
    hidden_two = jnp.tanh(vl_two[:own] + b2)
    lapin_two = vl_two[own:2 * own] + vl_two[2 * own:]
    slope_two = 1.0 - hidden_two * hidden_two
    bend_two = -2.0 * hidden_two * slope_two
    weight_s[...] = readout * slope_two

    def second(c, carry):
        block = x_two[pl.ds(c * CHUNK, CHUNK)].reshape(CHUNK * cols, width)
        folded = [0.0] * CHUNK
        for part in parts:
            grad = dot(block, w2[:, part])
            for i in range(CHUNK):
                row = c * CHUNK + i
                g = grad[i * cols:(i + 1) * cols]
                curv2_s[pl.ds(row, 1), part] = jnp.sum(g * g, axis=0, keepdims=True)
                terms = weight_s[pl.ds(row, 1), part] * g
                folded[i] += sum(terms[:, j:j + 128] for j in range(0, terms.shape[1], 128))
        for i in range(CHUNK):
            gbuf[pl.ds(c * CHUNK + i, 1), :] = jnp.sum(folded[i].T, axis=0, keepdims=True)
        return carry

    lax.fori_loop(0, chunks, second, 0)

    send(gbuf, grad_out.at[mine, :], gs, gr, partner)
    keep = pltpu.make_async_copy(gbuf, grad_out.at[mine, :], loc.at[len(local)])
    keep.start()
    gradient = gbuf[...]
    part = jnp.sum(
        readout * (slope_two * lapin_two + bend_two * curv2_s[...]), axis=1, keepdims=True
    ) + jnp.sum(gradient * gradient, axis=1, keepdims=True)
    amp = jnp.where(first_z, jnp.sum(readout * hidden_two, axis=1, keepdims=True), 0.0)
    lane = lax.broadcasted_iota(jnp.int32, (own, 128), 1)
    place = lane == lax.broadcasted_iota(jnp.int32, (own, 128), 0) + f * own
    kin_row = jnp.sum(jnp.where(place, part, 0.0), axis=0, keepdims=True)
    amp_row = jnp.sum(jnp.where(place, amp, 0.0), axis=0, keepdims=True)
    tile_row = lax.broadcasted_iota(jnp.int32, (8, 128), 0)
    msg[z, f] = jnp.where(tile_row == 0, amp_row, -0.5 * kin_row)
    slot = msg.at[z, f]
    others = [(k, g) for k in range(nz) for g in range(2) if k or g]
    for k, g in others:
        send(slot, slot, ms.at[k, g], mr.at[k, g], (w, z_at(k), other if g else f))
    for k, g in others:
        arrived(msg.at[z_at(k), other if g else f], ms.at[k, g], mr.at[k, g])
    total = msg[0, 0] + msg[0, 1]
    for k in range(1, nz):
        total = total + (msg[k, 0] + msg[k, 1])
    amp_out[...] = total[0:1, :2 * own]
    kin_out[...] = total[1:2, :2 * own]
    arrived(grad_out.at[theirs, :], gs, gr)
    keep.wait()
    for copy in sent:
        copy.wait_send()


def hand_over(*refs):
    sems = refs[-1]
    reads = [pltpu.make_async_copy(refs[i], refs[6 + i], sems.at[i]) for i in range(3)]
    writes = [pltpu.make_async_copy(refs[6 + i], refs[3 + i], sems.at[3 + i]) for i in range(3)]
    for copy in reads:
        copy.start()
    for read, write in zip(reads, writes):
        read.wait()
        write.start()
    for copy in writes:
        copy.wait()


def per_device(nw, nz, value_in, tang_in, lap_in, w_first, b_first, w_second, b_second, readout):
    walkers, cols, half = tang_in.shape
    width, own = 2 * half, walkers // 2
    shard = w_first.shape[0]
    gather = shard % 16 == 0
    if gather:
        w_shape = (nw, nz, 2, shard, width)
    else:
        w_shape = (width, width)
        w_first, w_second = (
            lax.all_gather(a, ("walker", "tangent", "feat"), axis=0, tiled=True) for a in (w_first, w_second)
        )
    chunks = own // CHUNK
    dma = pltpu.SemaphoreType.DMA
    in_hbm = pl.BlockSpec(memory_space=pltpu.HBM)
    in_vmem = pl.BlockSpec(memory_space=pltpu.VMEM)
    rows = own * cols
    row = jax.ShapeDtypeStruct((1, walkers), F32)
    results = pl.pallas_call(
        functools.partial(kernel, nw, nz, gather),
        out_shape=(jax.ShapeDtypeStruct((walkers, cols), F32), row, row),
        in_specs=[in_hbm] * 8,
        out_specs=(in_hbm, in_vmem, in_vmem),
        scratch_shapes=[
            pltpu.VMEM((own, cols, width), BF16),
            pltpu.VMEM((own, cols, width), BF16),
            pltpu.VMEM(w_shape, BF16),
            pltpu.VMEM(w_shape, BF16),
            pltpu.VMEM((2, own, width), BF16),
            pltpu.VMEM((3, 1, width), F32),
            pltpu.VMEM((own, width), F32),
            pltpu.VMEM((own, width), F32),
            pltpu.VMEM((own, width), F32),
            pltpu.VMEM((own, width), F32),
            pltpu.VMEM((own, cols), F32),
            pltpu.VMEM((nz, 2, 8, 128), F32),
            dma((8 + chunks,)),
            dma((2 + chunks,)),
            dma((2 + chunks,)),
            dma((2, nz)),
            dma((2, nz)),
            dma((nz, nw)),
            dma((nz, nw)),
            dma((nw,)),
            dma((nw,)),
            dma((nz,)),
            dma((nz,)),
            dma((nw,)),
            dma((nw,)),
            dma((nw,)),
            dma((nw,)),
            dma,
            dma,
            dma((nz, 2)),
            dma((nz, 2)),
        ],
        compiler_params=pltpu.CompilerParams(
            collective_id=0, has_side_effects=True, vmem_limit_bytes=64 * 2**20
        ),
        cost_estimate=pl.CostEstimate(
            flops=4 * rows * width * width, bytes_accessed=2 * rows * width, transcendentals=0
        ),
    )(
        value_in, tang_in, lap_in, w_first, b_first.reshape(1, width),
        w_second, b_second.reshape(1, width), readout.reshape(1, width),
    )
    grad, amp, kin = pl.pallas_call(
        hand_over,
        out_shape=[jax.ShapeDtypeStruct(a.shape, a.dtype) for a in results],
        in_specs=[in_hbm] * 3,
        out_specs=[in_hbm] * 3,
        scratch_shapes=[pltpu.VMEM(a.shape, a.dtype) for a in results] + [dma((6,))],
        compiler_params=pltpu.CompilerParams(vmem_limit_bytes=64 * 2**20),
    )(*results)
    return (amp.reshape(walkers), grad, kin.reshape(walkers))


def solution(mesh):
    placed = (
        P("walker", "feat"),
        P("walker", "tangent", "feat"),
        P("walker", "feat"),
        P(("walker", "tangent", "feat"), None),
        P(),
        P(("walker", "tangent", "feat"), None),
        P(),
        P(),
    )
    return jax.shard_map(
        functools.partial(per_device, mesh.shape["walker"], mesh.shape["tangent"]),
        mesh=mesh,
        in_specs=placed,
        out_specs=(P("walker"), P("walker", "tangent"), P("walker")),
        check_vma=False,
    )
```

```python
import functools

import jax
import jax.numpy as jnp
from jax import lax
from jax.experimental import pallas as pl
from jax.experimental.pallas import tpu as pltpu
from jax.sharding import PartitionSpec as P

F32 = jnp.float32
BF16 = jnp.bfloat16
MESH = pl.DeviceIdType.MESH
CHUNK = 8


def dot(a, b):
    return jnp.dot(a, b, preferred_element_type=F32)


def halves(a):
    high = a.astype(BF16)
    low = (a - high.astype(F32)).astype(BF16)
    return jnp.concatenate([high, low], axis=0)


def kernel(
    nw, nz, gather,
    value_ref, tang_ref, lap_ref, w1_ref, b1_ref, w2_ref, b2_ref, r_ref,
    grad_out, amp_out, kin_out,
    x, x_two, w1_all, w2_all, vl, vec, slope_s, weight_s, curv1_s, curv2_s, gbuf, msg,
    loc, ps, pr, za_s, za_r, wb_s, wb_r, wx_s, wx_r, fc_s, fc_r, vb_s, vb_r, vc_s, vc_r, gs, gr, ms, mr,
):
    w, z, f = lax.axis_index("walker"), lax.axis_index("tangent"), lax.axis_index("feat")
    other = 1 - f
    own, cols, width = x.shape
    half = width // 2
    parts = (slice(0, half), slice(half, width))
    chunks = own // CHUNK
    mine = pl.ds(pl.multiple_of(f * own, own), own)
    theirs = pl.ds(pl.multiple_of(other * own, own), own)
    my_cols = pl.ds(pl.multiple_of(f * half, half), half)
    their_cols = pl.ds(pl.multiple_of(other * half, half), half)
    partner = (w, z, other)

    def flipped(index, k):
        bit = 1
        while bit <= k:
            if (k // bit) % 2:
                index = index + bit - 2 * bit * lax.rem(lax.div(index, bit), 2)
            bit *= 2
        return index

    def z_at(k):
        return flipped(z, k)

    def w_at(k):
        return flipped(w, k)

    def remote(src, dst, send, recv, device):
        return pltpu.make_async_remote_copy(
            src_ref=src, dst_ref=dst, send_sem=send, recv_sem=recv, device_id=device, device_id_type=MESH
        )

    local = []

    def fetch(src, dst):
        copy = pltpu.make_async_copy(src, dst, loc.at[len(local)])
        copy.start()
        local.append(copy)
        return copy

    own_w = [
        fetch(src, dst.at[w, z, f] if gather else dst) for src, dst in ((w1_ref, w1_all), (w2_ref, w2_all))
    ]
    own_vec = [fetch(src, vec.at[i]) for i, src in enumerate((b1_ref, b2_ref, r_ref))]
    own_vl = [fetch(src.at[mine, :], vl.at[i, :, my_cols]) for i, src in enumerate((value_ref, lap_ref))]
    tang_at = len(local)
    for c in range(chunks):
        rows = pl.ds(f * own + c * CHUNK, CHUNK)
        fetch(tang_ref.at[rows], x.at[pl.ds(c * CHUNK, CHUNK), :, my_cols])

    barrier = pltpu.get_barrier_semaphore()
    greeted = [partner]
    for k in range(1, nz):
        greeted += [(w, z_at(k), f), (w, z_at(k), other)]
    if gather:
        for k in range(1, nw):
            greeted += [(w_at(k), z, f), (w_at(k), z, other)]
    for device in greeted:
        pl.semaphore_signal(barrier, inc=1, device_id=device, device_id_type=MESH)
    if gather:
        for copy in own_w:
            copy.wait()
    pl.semaphore_wait(barrier, len(greeted))

    sent = []

    def send(*args):
        copy = remote(*args)
        copy.start()
        sent.append(copy)

    def arrived(ref, send_sem, recv_sem):
        remote(ref, ref, send_sem, recv_sem, partner).wait_recv()

    weights = (w1_all, w2_all)

    def along_z(layer):
        piece = weights[layer].at[w, z, f]
        for k in range(1, nz):
            send(piece, piece, za_s.at[layer, k], za_r.at[layer, k], (w, z_at(k), f))

    def from_z(layer, k):
        arrived(weights[layer].at[w, z_at(k), f], za_s.at[layer, k], za_r.at[layer, k])

    def pass_across(k):
        piece = w1_all.at[w, z_at(k), f]
        for j in range(1, nw):
            send(piece, piece, wb_s.at[k, j], wb_r.at[k, j], (w_at(j), z, f))
        if k == nz - 1:
            for j in range(nw):
                send(piece, piece, wx_s.at[j], wx_r.at[j], (w_at(j), z, other))

    def pass_over(k):
        for j in range(1, nw):
            arrived(w1_all.at[w_at(j), z_at(k), f], wb_s.at[k, j], wb_r.at[k, j])
        if k < nz - 1:
            piece = w1_all.at[:, z_at(k), f]
            send(piece, piece, fc_s.at[k], fc_r.at[k], partner)

    def second_across():
        piece = w2_all.at[w, :, f]
        for j in range(1, nw):
            send(piece, piece, vb_s.at[j], vb_r.at[j], (w_at(j), z, f))

    def second_over(j):
        piece = w2_all.at[w_at(j), :, f]
        if j:
            arrived(piece, vb_s.at[j], vb_r.at[j])
        send(piece, piece, vc_s.at[j], vc_r.at[j], partner)

    def whole(layer):
        dst = weights[layer]
        if not gather:
            own_w[layer].wait()
        elif layer == 0:
            for k in range(nz - 1):
                arrived(dst.at[:, z_at(k), other], fc_s.at[k], fc_r.at[k])
            for j in range(nw):
                arrived(dst.at[w_at(j), z_at(nz - 1), other], wx_s.at[j], wx_r.at[j])
        else:
            for j in range(nw):
                arrived(dst.at[w_at(j), :, other], vc_s.at[j], vc_r.at[j])
        return dst[...].reshape(width, width)

    def give(c):
        rows = pl.ds(other * own + c * CHUNK, CHUNK)
        send(
            tang_ref.at[rows], x.at[pl.ds(c * CHUNK, CHUNK), :, my_cols],
            ps.at[2 + c], pr.at[2 + c], partner,
        )

    if gather:
        along_z(0)
        pass_across(0)
    for i, src in enumerate((value_ref, lap_ref)):
        send(src.at[theirs, :], vl.at[i, :, my_cols], ps.at[i], pr.at[i], partner)
    if gather:
        along_z(1)
    for c in range(chunks):
        give(c)
    if gather:
        for k in range(1, nz):
            from_z(0, k)
            pass_across(k)
            pass_over(k - 1)
        for k in range(1, nz):
            from_z(1, k)
        second_across()
        pass_over(nz - 1)
        second_over(0)

    for copy in own_vec + own_vl:
        copy.wait()
    for i in range(2):
        arrived(vl.at[i, :, their_cols], ps.at[i], pr.at[i])
    b1, b2, readout = vec[0], vec[1], vec[2]

    w1 = whole(0)
    vl_one = dot(vl[...].reshape(2 * own, width), w1)
    hidden_one = jnp.tanh(vl_one[:own] + b1)
    lapin_one = vl_one[own:]
    slope_one = 1.0 - hidden_one * hidden_one
    bend_one = -2.0 * hidden_one * slope_one
    slope_s[...] = slope_one

    def first(c, carry):
        own_part = x.at[pl.ds(c * CHUNK, CHUNK), :, my_cols]
        pltpu.make_async_copy(own_part, own_part, loc.at[tang_at + c]).wait()
        arrived(x.at[pl.ds(c * CHUNK, CHUNK), :, their_cols], ps.at[2 + c], pr.at[2 + c])
        block = x[pl.ds(c * CHUNK, CHUNK)].reshape(CHUNK * cols, width)
        for part in parts:
            grad = dot(block, w1[:, part])
            for i in range(CHUNK):
                row = c * CHUNK + i
                g = grad[i * cols:(i + 1) * cols]
                curv1_s[pl.ds(row, 1), part] = jnp.sum(g * g, axis=0, keepdims=True)
                x_two[row, :, part] = (slope_s[pl.ds(row, 1), part] * g).astype(BF16)
        return carry

    lax.fori_loop(0, chunks - 1, first, 0)
    if gather:
        for j in range(1, nw):
            second_over(j)
    first(chunks - 1, 0)

    w2 = whole(1)
    first_z = z == 0
    lap_two = bend_one * curv1_s[...] + jnp.where(first_z, slope_one * lapin_one, 0.0)
    vl_two = dot(jnp.concatenate([hidden_one.astype(BF16), halves(lap_two)], axis=0), w2)
    hidden_two = jnp.tanh(vl_two[:own] + b2)
    lapin_two = vl_two[own:2 * own] + vl_two[2 * own:]
    slope_two = 1.0 - hidden_two * hidden_two
    bend_two = -2.0 * hidden_two * slope_two
    weight_s[...] = readout * slope_two

    def second(c, carry):
        block = x_two[pl.ds(c * CHUNK, CHUNK)].reshape(CHUNK * cols, width)
        folded = [0.0] * CHUNK
        for part in parts:
            grad = dot(block, w2[:, part])
            for i in range(CHUNK):
                row = c * CHUNK + i
                g = grad[i * cols:(i + 1) * cols]
                curv2_s[pl.ds(row, 1), part] = jnp.sum(g * g, axis=0, keepdims=True)
                terms = weight_s[pl.ds(row, 1), part] * g
                folded[i] += sum(terms[:, j:j + 128] for j in range(0, terms.shape[1], 128))
        terms = jnp.concatenate(folded, axis=0)
        high = terms.astype(BF16)
        low = (terms - high.astype(F32)).astype(BF16)
        sums = dot(jnp.concatenate([high, low], axis=1), jnp.ones((256, 128), BF16))
        for i in range(CHUNK):
            here = walker_lane == c * CHUNK + i
            carry = carry + jnp.where(here, sums[i * cols:(i + 1) * cols], 0.0)
        return carry

    walker_lane = lax.broadcasted_iota(jnp.int32, (cols, 128), 1)
    gradient = lax.fori_loop(0, chunks, second, jnp.zeros((cols, 128), F32)).T[:own]
    gbuf[...] = gradient

    send(gbuf, grad_out.at[mine, :], gs, gr, partner)
    keep = pltpu.make_async_copy(gbuf, grad_out.at[mine, :], loc.at[len(local)])
    keep.start()
    part = jnp.sum(
        readout * (slope_two * lapin_two + bend_two * curv2_s[...]), axis=1, keepdims=True
    ) + jnp.sum(gradient * gradient, axis=1, keepdims=True)
    amp = jnp.where(first_z, jnp.sum(readout * hidden_two, axis=1, keepdims=True), 0.0)
    lane = lax.broadcasted_iota(jnp.int32, (own, 128), 1)
    place = lane == lax.broadcasted_iota(jnp.int32, (own, 128), 0) + f * own
    kin_row = jnp.sum(jnp.where(place, part, 0.0), axis=0, keepdims=True)
    amp_row = jnp.sum(jnp.where(place, amp, 0.0), axis=0, keepdims=True)
    tile_row = lax.broadcasted_iota(jnp.int32, (8, 128), 0)
    msg[z, f] = jnp.where(tile_row == 0, amp_row, -0.5 * kin_row)
    slot = msg.at[z, f]
    others = [(k, g) for k in range(nz) for g in range(2) if k or g]
    for k, g in others:
        send(slot, slot, ms.at[k, g], mr.at[k, g], (w, z_at(k), other if g else f))
    for k, g in others:
        arrived(msg.at[z_at(k), other if g else f], ms.at[k, g], mr.at[k, g])
    total = msg[0, 0] + msg[0, 1]
    for k in range(1, nz):
        total = total + (msg[k, 0] + msg[k, 1])
    amp_out[...] = total[0:1, :2 * own]
    kin_out[...] = total[1:2, :2 * own]
    arrived(grad_out.at[theirs, :], gs, gr)
    keep.wait()
    for copy in sent:
        copy.wait_send()


def hand_over(*refs):
    sems = refs[-1]
    reads = [pltpu.make_async_copy(refs[i], refs[6 + i], sems.at[i]) for i in range(3)]
    writes = [pltpu.make_async_copy(refs[6 + i], refs[3 + i], sems.at[3 + i]) for i in range(3)]
    for copy in reads:
        copy.start()
    for read, write in zip(reads, writes):
        read.wait()
        write.start()
    for copy in writes:
        copy.wait()


def per_device(nw, nz, value_in, tang_in, lap_in, w_first, b_first, w_second, b_second, readout):
    walkers, cols, half = tang_in.shape
    width, own = 2 * half, walkers // 2
    shard = w_first.shape[0]
    gather = shard % 16 == 0
    if gather:
        w_shape = (nw, nz, 2, shard, width)
    else:
        w_shape = (width, width)
        w_first, w_second = (
            lax.all_gather(a, ("walker", "tangent", "feat"), axis=0, tiled=True) for a in (w_first, w_second)
        )
    chunks = own // CHUNK
    dma = pltpu.SemaphoreType.DMA
    in_hbm = pl.BlockSpec(memory_space=pltpu.HBM)
    in_vmem = pl.BlockSpec(memory_space=pltpu.VMEM)
    rows = own * cols
    row = jax.ShapeDtypeStruct((1, walkers), F32)
    results = pl.pallas_call(
        functools.partial(kernel, nw, nz, gather),
        out_shape=(jax.ShapeDtypeStruct((walkers, cols), F32), row, row),
        in_specs=[in_hbm] * 8,
        out_specs=(in_hbm, in_vmem, in_vmem),
        scratch_shapes=[
            pltpu.VMEM((own, cols, width), BF16),
            pltpu.VMEM((own, cols, width), BF16),
            pltpu.VMEM(w_shape, BF16),
            pltpu.VMEM(w_shape, BF16),
            pltpu.VMEM((2, own, width), BF16),
            pltpu.VMEM((3, 1, width), F32),
            pltpu.VMEM((own, width), F32),
            pltpu.VMEM((own, width), F32),
            pltpu.VMEM((own, width), F32),
            pltpu.VMEM((own, width), F32),
            pltpu.VMEM((own, cols), F32),
            pltpu.VMEM((nz, 2, 8, 128), F32),
            dma((8 + chunks,)),
            dma((2 + chunks,)),
            dma((2 + chunks,)),
            dma((2, nz)),
            dma((2, nz)),
            dma((nz, nw)),
            dma((nz, nw)),
            dma((nw,)),
            dma((nw,)),
            dma((nz,)),
            dma((nz,)),
            dma((nw,)),
            dma((nw,)),
            dma((nw,)),
            dma((nw,)),
            dma,
            dma,
            dma((nz, 2)),
            dma((nz, 2)),
        ],
        compiler_params=pltpu.CompilerParams(
            collective_id=0, has_side_effects=True, vmem_limit_bytes=64 * 2**20
        ),
        cost_estimate=pl.CostEstimate(
            flops=4 * rows * width * width, bytes_accessed=2 * rows * width, transcendentals=0
        ),
    )(
        value_in, tang_in, lap_in, w_first, b_first.reshape(1, width),
        w_second, b_second.reshape(1, width), readout.reshape(1, width),
    )
    grad, amp, kin = pl.pallas_call(
        hand_over,
        out_shape=[jax.ShapeDtypeStruct(a.shape, a.dtype) for a in results],
        in_specs=[in_hbm] * 3,
        out_specs=[in_hbm] * 3,
        scratch_shapes=[pltpu.VMEM(a.shape, a.dtype) for a in results] + [dma((6,))],
        compiler_params=pltpu.CompilerParams(vmem_limit_bytes=64 * 2**20),
    )(*results)
    return (amp.reshape(walkers), grad, kin.reshape(walkers))


def solution(mesh):
    placed = (
        P("walker", "feat"),
        P("walker", "tangent", "feat"),
        P("walker", "feat"),
        P(("walker", "tangent", "feat"), None),
        P(),
        P(("walker", "tangent", "feat"), None),
        P(),
        P(),
    )
    return jax.shard_map(
        functools.partial(per_device, mesh.shape["walker"], mesh.shape["tangent"]),
        mesh=mesh,
        in_specs=placed,
        out_specs=(P("walker"), P("walker", "tangent"), P("walker")),
        check_vma=False,
    )
```

```python
import functools

import jax
import jax.numpy as jnp
from jax import lax
from jax.experimental import pallas as pl
from jax.experimental.pallas import tpu as pltpu
from jax.sharding import PartitionSpec as P

F32 = jnp.float32
BF16 = jnp.bfloat16
MESH = pl.DeviceIdType.MESH
CHUNK = 4


def dot(a, b):
    return jnp.dot(a, b, preferred_element_type=F32)


def halves(a):
    high = a.astype(BF16)
    low = (a - high.astype(F32)).astype(BF16)
    return jnp.concatenate([high, low], axis=0)


def kernel(
    nw, nz, gather,
    value_ref, tang_ref, lap_ref, w1_ref, b1_ref, w2_ref, b2_ref, r_ref,
    grad_out, amp_out, kin_out,
    x, x_two, w1_all, w2_all, vl, vec, slope_s, weight_s, curv1_s, curv2_s, gbuf, msg,
    loc, ps, pr, za_s, za_r, wb_s, wb_r, wx_s, wx_r, fc_s, fc_r, vb_s, vb_r, vc_s, vc_r, gs, gr, ms, mr,
):
    w, z, f = lax.axis_index("walker"), lax.axis_index("tangent"), lax.axis_index("feat")
    other = 1 - f
    own, cols, width = x.shape
    half = width // 2
    parts = (slice(0, half), slice(half, width))
    chunks = own // CHUNK
    mine = pl.ds(pl.multiple_of(f * own, own), own)
    theirs = pl.ds(pl.multiple_of(other * own, own), own)
    my_cols = pl.ds(pl.multiple_of(f * half, half), half)
    their_cols = pl.ds(pl.multiple_of(other * half, half), half)
    partner = (w, z, other)

    def flipped(index, k):
        bit = 1
        while bit <= k:
            if (k // bit) % 2:
                index = index + bit - 2 * bit * lax.rem(lax.div(index, bit), 2)
            bit *= 2
        return index

    def z_at(k):
        return flipped(z, k)

    def w_at(k):
        return flipped(w, k)

    def remote(src, dst, send, recv, device):
        return pltpu.make_async_remote_copy(
            src_ref=src, dst_ref=dst, send_sem=send, recv_sem=recv, device_id=device, device_id_type=MESH
        )

    local = []

    def fetch(src, dst):
        copy = pltpu.make_async_copy(src, dst, loc.at[len(local)])
        copy.start()
        local.append(copy)
        return copy

    own_w = [
        fetch(src, dst.at[w, z, f] if gather else dst) for src, dst in ((w1_ref, w1_all), (w2_ref, w2_all))
    ]
    own_vec = [fetch(src, vec.at[i]) for i, src in enumerate((b1_ref, b2_ref, r_ref))]
    own_vl = [fetch(src.at[mine, :], vl.at[i, :, my_cols]) for i, src in enumerate((value_ref, lap_ref))]
    tang_at = len(local)
    for c in range(chunks):
        rows = pl.ds(f * own + c * CHUNK, CHUNK)
        fetch(tang_ref.at[rows], x.at[pl.ds(c * CHUNK, CHUNK), :, my_cols])

    barrier = pltpu.get_barrier_semaphore()
    greeted = [partner]
    for k in range(1, nz):
        greeted += [(w, z_at(k), f), (w, z_at(k), other)]
    if gather:
        for k in range(1, nw):
            greeted += [(w_at(k), z, f), (w_at(k), z, other)]
    for device in greeted:
        pl.semaphore_signal(barrier, inc=1, device_id=device, device_id_type=MESH)
    if gather:
        for copy in own_w:
            copy.wait()
    pl.semaphore_wait(barrier, len(greeted))

    sent = []

    def send(*args):
        copy = remote(*args)
        copy.start()
        sent.append(copy)

    def arrived(ref, send_sem, recv_sem):
        remote(ref, ref, send_sem, recv_sem, partner).wait_recv()

    weights = (w1_all, w2_all)

    def along_z(layer):
        piece = weights[layer].at[w, z, f]
        for k in range(1, nz):
            send(piece, piece, za_s.at[layer, k], za_r.at[layer, k], (w, z_at(k), f))

    def from_z(layer, k):
        arrived(weights[layer].at[w, z_at(k), f], za_s.at[layer, k], za_r.at[layer, k])

    def pass_across(k):
        piece = w1_all.at[w, z_at(k), f]
        for j in range(1, nw):
            send(piece, piece, wb_s.at[k, j], wb_r.at[k, j], (w_at(j), z, f))
        if k == nz - 1:
            for j in range(nw):
                send(piece, piece, wx_s.at[j], wx_r.at[j], (w_at(j), z, other))

    def pass_over(k):
        for j in range(1, nw):
            arrived(w1_all.at[w_at(j), z_at(k), f], wb_s.at[k, j], wb_r.at[k, j])
        if k < nz - 1:
            piece = w1_all.at[:, z_at(k), f]
            send(piece, piece, fc_s.at[k], fc_r.at[k], partner)

    def second_across():
        piece = w2_all.at[w, :, f]
        for j in range(1, nw):
            send(piece, piece, vb_s.at[j], vb_r.at[j], (w_at(j), z, f))

    def second_over(j):
        piece = w2_all.at[w_at(j), :, f]
        if j:
            arrived(piece, vb_s.at[j], vb_r.at[j])
        send(piece, piece, vc_s.at[j], vc_r.at[j], partner)

    def whole(layer):
        dst = weights[layer]
        if not gather:
            own_w[layer].wait()
        elif layer == 0:
            for k in range(nz - 1):
                arrived(dst.at[:, z_at(k), other], fc_s.at[k], fc_r.at[k])
            for j in range(nw):
                arrived(dst.at[w_at(j), z_at(nz - 1), other], wx_s.at[j], wx_r.at[j])
        else:
            for j in range(nw):
                arrived(dst.at[w_at(j), :, other], vc_s.at[j], vc_r.at[j])
        return dst[...].reshape(width, width)

    def give(c):
        rows = pl.ds(other * own + c * CHUNK, CHUNK)
        send(
            tang_ref.at[rows], x.at[pl.ds(c * CHUNK, CHUNK), :, my_cols],
            ps.at[2 + c], pr.at[2 + c], partner,
        )

    if gather:
        along_z(0)
        pass_across(0)
    for i, src in enumerate((value_ref, lap_ref)):
        send(src.at[theirs, :], vl.at[i, :, my_cols], ps.at[i], pr.at[i], partner)
    if gather:
        along_z(1)
    for c in range(chunks):
        give(c)
    if gather:
        for k in range(1, nz):
            from_z(0, k)
            pass_across(k)
            if k < nz - 1:
                pass_over(k - 1)
        for k in range(1, nz):
            from_z(1, k)
        second_across()
        pass_over(nz - 2)
        pass_over(nz - 1)
        second_over(0)

    for copy in own_vec + own_vl:
        copy.wait()
    for i in range(2):
        arrived(vl.at[i, :, their_cols], ps.at[i], pr.at[i])
    b1, b2, readout = vec[0], vec[1], vec[2]

    w1 = whole(0)
    vl_one = dot(vl[...].reshape(2 * own, width), w1)
    hidden_one = jnp.tanh(vl_one[:own] + b1)
    lapin_one = vl_one[own:]
    slope_one = 1.0 - hidden_one * hidden_one
    bend_one = -2.0 * hidden_one * slope_one
    slope_s[...] = slope_one

    def first(c, carry):
        own_part = x.at[pl.ds(c * CHUNK, CHUNK), :, my_cols]
        pltpu.make_async_copy(own_part, own_part, loc.at[tang_at + c]).wait()
        arrived(x.at[pl.ds(c * CHUNK, CHUNK), :, their_cols], ps.at[2 + c], pr.at[2 + c])
        block = x[pl.ds(c * CHUNK, CHUNK)].reshape(CHUNK * cols, width)
        for part in parts:
            grad = dot(block, w1[:, part])
            for i in range(CHUNK):
                row = c * CHUNK + i
                g = grad[i * cols:(i + 1) * cols]
                curv1_s[pl.ds(row, 1), part] = jnp.sum(g * g, axis=0, keepdims=True)
                x_two[row, :, part] = (slope_s[pl.ds(row, 1), part] * g).astype(BF16)
        return carry

    lax.fori_loop(0, chunks // 2, first, 0)
    if gather:
        for j in range(1, nw):
            second_over(j)
    lax.fori_loop(chunks // 2, chunks, first, 0)

    w2 = whole(1)
    first_z = z == 0
    lap_two = bend_one * curv1_s[...] + jnp.where(first_z, slope_one * lapin_one, 0.0)
    vl_two = dot(jnp.concatenate([hidden_one.astype(BF16), halves(lap_two)], axis=0), w2)
    hidden_two = jnp.tanh(vl_two[:own] + b2)
    lapin_two = vl_two[own:2 * own] + vl_two[2 * own:]
    slope_two = 1.0 - hidden_two * hidden_two
    bend_two = -2.0 * hidden_two * slope_two
    weight_s[...] = readout * slope_two

    def second(c, carry):
        block = x_two[pl.ds(c * CHUNK, CHUNK)].reshape(CHUNK * cols, width)
        folded = [0.0] * CHUNK
        for part in parts:
            grad = dot(block, w2[:, part])
            for i in range(CHUNK):
                row = c * CHUNK + i
                g = grad[i * cols:(i + 1) * cols]
                curv2_s[pl.ds(row, 1), part] = jnp.sum(g * g, axis=0, keepdims=True)
                terms = weight_s[pl.ds(row, 1), part] * g
                folded[i] += sum(terms[:, j:j + 128] for j in range(0, terms.shape[1], 128))
        terms = jnp.concatenate(folded, axis=0)
        high = terms.astype(BF16)
        low = (terms - high.astype(F32)).astype(BF16)
        sums = dot(jnp.concatenate([high, low], axis=1), jnp.ones((256, 128), BF16))
        for i in range(CHUNK):
            here = walker_lane == c * CHUNK + i
            carry = carry + jnp.where(here, sums[i * cols:(i + 1) * cols], 0.0)
        return carry

    walker_lane = lax.broadcasted_iota(jnp.int32, (cols, 128), 1)
    gradient = lax.fori_loop(0, chunks, second, jnp.zeros((cols, 128), F32)).T[:own]
    gbuf[...] = gradient

    send(gbuf, grad_out.at[mine, :], gs, gr, partner)
    keep = pltpu.make_async_copy(gbuf, grad_out.at[mine, :], loc.at[len(local)])
    keep.start()
    part = jnp.sum(
        readout * (slope_two * lapin_two + bend_two * curv2_s[...]), axis=1, keepdims=True
    ) + jnp.sum(gradient * gradient, axis=1, keepdims=True)
    amp = jnp.where(first_z, jnp.sum(readout * hidden_two, axis=1, keepdims=True), 0.0)
    lane = lax.broadcasted_iota(jnp.int32, (own, 128), 1)
    place = lane == lax.broadcasted_iota(jnp.int32, (own, 128), 0) + f * own
    kin_row = jnp.sum(jnp.where(place, part, 0.0), axis=0, keepdims=True)
    amp_row = jnp.sum(jnp.where(place, amp, 0.0), axis=0, keepdims=True)
    tile_row = lax.broadcasted_iota(jnp.int32, (8, 128), 0)
    msg[z, f] = jnp.where(tile_row == 0, amp_row, -0.5 * kin_row)
    slot = msg.at[z, f]
    others = [(k, g) for k in range(nz) for g in range(2) if k or g]
    for k, g in others:
        send(slot, slot, ms.at[k, g], mr.at[k, g], (w, z_at(k), other if g else f))
    for k, g in others:
        arrived(msg.at[z_at(k), other if g else f], ms.at[k, g], mr.at[k, g])
    total = msg[0, 0] + msg[0, 1]
    for k in range(1, nz):
        total = total + (msg[k, 0] + msg[k, 1])
    amp_out[...] = total[0:1, :2 * own]
    kin_out[...] = total[1:2, :2 * own]
    arrived(grad_out.at[theirs, :], gs, gr)
    keep.wait()
    for copy in sent:
        copy.wait_send()


def hand_over(*refs):
    sems = refs[-1]
    reads = [pltpu.make_async_copy(refs[i], refs[6 + i], sems.at[i]) for i in range(3)]
    writes = [pltpu.make_async_copy(refs[6 + i], refs[3 + i], sems.at[3 + i]) for i in range(3)]
    for copy in reads:
        copy.start()
    for read, write in zip(reads, writes):
        read.wait()
        write.start()
    for copy in writes:
        copy.wait()


def per_device(nw, nz, value_in, tang_in, lap_in, w_first, b_first, w_second, b_second, readout):
    walkers, cols, half = tang_in.shape
    width, own = 2 * half, walkers // 2
    shard = w_first.shape[0]
    gather = shard % 16 == 0
    if gather:
        w_shape = (nw, nz, 2, shard, width)
    else:
        w_shape = (width, width)
        w_first, w_second = (
            lax.all_gather(a, ("walker", "tangent", "feat"), axis=0, tiled=True) for a in (w_first, w_second)
        )
    chunks = own // CHUNK
    dma = pltpu.SemaphoreType.DMA
    in_hbm = pl.BlockSpec(memory_space=pltpu.HBM)
    in_vmem = pl.BlockSpec(memory_space=pltpu.VMEM)
    rows = own * cols
    row = jax.ShapeDtypeStruct((1, walkers), F32)
    results = pl.pallas_call(
        functools.partial(kernel, nw, nz, gather),
        out_shape=(jax.ShapeDtypeStruct((walkers, cols), F32), row, row),
        in_specs=[in_hbm] * 8,
        out_specs=(in_hbm, in_vmem, in_vmem),
        scratch_shapes=[
            pltpu.VMEM((own, cols, width), BF16),
            pltpu.VMEM((own, cols, width), BF16),
            pltpu.VMEM(w_shape, BF16),
            pltpu.VMEM(w_shape, BF16),
            pltpu.VMEM((2, own, width), BF16),
            pltpu.VMEM((3, 1, width), F32),
            pltpu.VMEM((own, width), F32),
            pltpu.VMEM((own, width), F32),
            pltpu.VMEM((own, width), F32),
            pltpu.VMEM((own, width), F32),
            pltpu.VMEM((own, cols), F32),
            pltpu.VMEM((nz, 2, 8, 128), F32),
            dma((8 + chunks,)),
            dma((2 + chunks,)),
            dma((2 + chunks,)),
            dma((2, nz)),
            dma((2, nz)),
            dma((nz, nw)),
            dma((nz, nw)),
            dma((nw,)),
            dma((nw,)),
            dma((nz,)),
            dma((nz,)),
            dma((nw,)),
            dma((nw,)),
            dma((nw,)),
            dma((nw,)),
            dma,
            dma,
            dma((nz, 2)),
            dma((nz, 2)),
        ],
        compiler_params=pltpu.CompilerParams(
            collective_id=0, has_side_effects=True, vmem_limit_bytes=64 * 2**20
        ),
        cost_estimate=pl.CostEstimate(
            flops=4 * rows * width * width, bytes_accessed=2 * rows * width, transcendentals=0
        ),
    )(
        value_in, tang_in, lap_in, w_first, b_first.reshape(1, width),
        w_second, b_second.reshape(1, width), readout.reshape(1, width),
    )
    grad, amp, kin = pl.pallas_call(
        hand_over,
        out_shape=[jax.ShapeDtypeStruct(a.shape, a.dtype) for a in results],
        in_specs=[in_hbm] * 3,
        out_specs=[in_hbm] * 3,
        scratch_shapes=[pltpu.VMEM(a.shape, a.dtype) for a in results] + [dma((6,))],
        compiler_params=pltpu.CompilerParams(vmem_limit_bytes=64 * 2**20),
    )(*results)
    return (amp.reshape(walkers), grad, kin.reshape(walkers))


def solution(mesh):
    placed = (
        P("walker", "feat"),
        P("walker", "tangent", "feat"),
        P("walker", "feat"),
        P(("walker", "tangent", "feat"), None),
        P(),
        P(("walker", "tangent", "feat"), None),
        P(),
        P(),
    )
    return jax.shard_map(
        functools.partial(per_device, mesh.shape["walker"], mesh.shape["tangent"]),
        mesh=mesh,
        in_specs=placed,
        out_specs=(P("walker"), P("walker", "tangent"), P("walker")),
        check_vma=False,
    )
```

```python
import functools

import jax
import jax.numpy as jnp
from jax import lax
from jax.experimental import pallas as pl
from jax.experimental.pallas import tpu as pltpu
from jax.sharding import PartitionSpec as P

F32 = jnp.float32
BF16 = jnp.bfloat16
MESH = pl.DeviceIdType.MESH
CHUNK = 8


def dot(a, b):
    return jnp.dot(a, b, preferred_element_type=F32)


def halves(a):
    high = a.astype(BF16)
    low = (a - high.astype(F32)).astype(BF16)
    return jnp.concatenate([high, low], axis=0)


def kernel(
    nw, nz, gather,
    value_ref, tang_ref, lap_ref, w1_ref, b1_ref, w2_ref, b2_ref, r_ref,
    grad_out, amp_out, kin_out,
    x, x_two, w1_all, w2_all, vl, vec, slope_s, weight_s, curv1_s, curv2_s, gbuf, msg,
    loc, ps, pr, za_s, za_r, wb_s, wb_r, wx_s, wx_r, fc_s, fc_r, vb_s, vb_r, vc_s, vc_r, gs, gr, ms, mr,
):
    w, z, f = lax.axis_index("walker"), lax.axis_index("tangent"), lax.axis_index("feat")
    other = 1 - f
    own, cols, width = x.shape
    half = width // 2
    parts = (slice(0, half), slice(half, width))
    chunks = own // CHUNK
    mine = pl.ds(pl.multiple_of(f * own, own), own)
    theirs = pl.ds(pl.multiple_of(other * own, own), own)
    my_cols = pl.ds(pl.multiple_of(f * half, half), half)
    their_cols = pl.ds(pl.multiple_of(other * half, half), half)
    partner = (w, z, other)

    def flipped(index, k):
        bit = 1
        while bit <= k:
            if (k // bit) % 2:
                index = index + bit - 2 * bit * lax.rem(lax.div(index, bit), 2)
            bit *= 2
        return index

    def z_at(k):
        return flipped(z, k)

    def w_at(k):
        return flipped(w, k)

    def remote(src, dst, send, recv, device):
        return pltpu.make_async_remote_copy(
            src_ref=src, dst_ref=dst, send_sem=send, recv_sem=recv, device_id=device, device_id_type=MESH
        )

    local = []

    def fetch(src, dst):
        copy = pltpu.make_async_copy(src, dst, loc.at[len(local)])
        copy.start()
        local.append(copy)
        return copy

    own_w = [
        fetch(src, dst.at[w, z, f] if gather else dst) for src, dst in ((w1_ref, w1_all), (w2_ref, w2_all))
    ]
    own_vec = [fetch(src, vec.at[i]) for i, src in enumerate((b1_ref, b2_ref, r_ref))]
    own_vl = [fetch(src.at[mine, :], vl.at[i, :, my_cols]) for i, src in enumerate((value_ref, lap_ref))]
    tang_at = len(local)
    for c in range(chunks):
        rows = pl.ds(f * own + c * CHUNK, CHUNK)
        fetch(tang_ref.at[rows], x.at[pl.ds(c * CHUNK, CHUNK), :, my_cols])

    barrier = pltpu.get_barrier_semaphore()
    greeted = [partner]
    for k in range(1, nz):
        greeted += [(w, z_at(k), f), (w, z_at(k), other)]
    if gather:
        for k in range(1, nw):
            greeted += [(w_at(k), z, f), (w_at(k), z, other)]
    for device in greeted:
        pl.semaphore_signal(barrier, inc=1, device_id=device, device_id_type=MESH)
    if gather:
        for copy in own_w:
            copy.wait()
    pl.semaphore_wait(barrier, len(greeted))

    sent = []

    def send(*args):
        copy = remote(*args)
        copy.start()
        sent.append(copy)

    def arrived(ref, send_sem, recv_sem):
        remote(ref, ref, send_sem, recv_sem, partner).wait_recv()

    weights = (w1_all, w2_all)

    def along_z(layer):
        piece = weights[layer].at[w, z, f]
        for k in range(1, nz):
            send(piece, piece, za_s.at[layer, k], za_r.at[layer, k], (w, z_at(k), f))

    def from_z(layer, k):
        arrived(weights[layer].at[w, z_at(k), f], za_s.at[layer, k], za_r.at[layer, k])

    def pass_across(k):
        piece = w1_all.at[w, z_at(k), f]
        for j in range(1, nw):
            send(piece, piece, wb_s.at[k, j], wb_r.at[k, j], (w_at(j), z, f))
        if k == nz - 1:
            for j in range(nw):
                send(piece, piece, wx_s.at[j], wx_r.at[j], (w_at(j), z, other))

    def pass_over(k):
        for j in range(1, nw):
            arrived(w1_all.at[w_at(j), z_at(k), f], wb_s.at[k, j], wb_r.at[k, j])
        if k < nz - 1:
            piece = w1_all.at[:, z_at(k), f]
            send(piece, piece, fc_s.at[k], fc_r.at[k], partner)

    def second_across():
        piece = w2_all.at[w, :, f]
        for j in range(1, nw):
            send(piece, piece, vb_s.at[j], vb_r.at[j], (w_at(j), z, f))

    def second_over(j):
        piece = w2_all.at[w_at(j), :, f]
        if j:
            arrived(piece, vb_s.at[j], vb_r.at[j])
        send(piece, piece, vc_s.at[j], vc_r.at[j], partner)

    def whole(layer):
        dst = weights[layer]
        if not gather:
            own_w[layer].wait()
        elif layer == 0:
            for k in range(nz - 1):
                arrived(dst.at[:, z_at(k), other], fc_s.at[k], fc_r.at[k])
            for j in range(nw):
                arrived(dst.at[w_at(j), z_at(nz - 1), other], wx_s.at[j], wx_r.at[j])
        else:
            for j in range(nw):
                arrived(dst.at[w_at(j), :, other], vc_s.at[j], vc_r.at[j])
        return dst[...].reshape(width, width)

    def give(c):
        rows = pl.ds(other * own + c * CHUNK, CHUNK)
        send(
            tang_ref.at[rows], x.at[pl.ds(c * CHUNK, CHUNK), :, my_cols],
            ps.at[2 + c], pr.at[2 + c], partner,
        )

    if gather:
        along_z(0)
        pass_across(0)
    for i, src in enumerate((value_ref, lap_ref)):
        send(src.at[theirs, :], vl.at[i, :, my_cols], ps.at[i], pr.at[i], partner)
    if gather:
        along_z(1)
    for c in range(chunks):
        give(c)
    if gather:
        for k in range(1, nz):
            from_z(0, k)
            pass_across(k)
            pass_over(k - 1)
        for k in range(1, nz):
            from_z(1, k)
        second_across()
        pass_over(nz - 1)
        second_over(0)

    for copy in own_vec + own_vl:
        copy.wait()
    for i in range(2):
        arrived(vl.at[i, :, their_cols], ps.at[i], pr.at[i])
    b1, b2, readout = vec[0], vec[1], vec[2]

    def tangents_here(c):
        own_part = x.at[pl.ds(c * CHUNK, CHUNK), :, my_cols]
        pltpu.make_async_copy(own_part, own_part, loc.at[tang_at + c]).wait()
        arrived(x.at[pl.ds(c * CHUNK, CHUNK), :, their_cols], ps.at[2 + c], pr.at[2 + c])

    tangents_here(0)
    w1 = whole(0)
    vl_one = dot(vl[...].reshape(2 * own, width), w1)
    hidden_one = jnp.tanh(vl_one[:own] + b1)
    lapin_one = vl_one[own:]
    slope_one = 1.0 - hidden_one * hidden_one
    bend_one = -2.0 * hidden_one * slope_one
    slope_s[...] = slope_one

    def first(c):
        block = x[pl.ds(c * CHUNK, CHUNK)].reshape(CHUNK * cols, width)
        for part in parts:
            grad = dot(block, w1[:, part])
            for i in range(CHUNK):
                row = c * CHUNK + i
                g = grad[i * cols:(i + 1) * cols]
                curv1_s[pl.ds(row, 1), part] = jnp.sum(g * g, axis=0, keepdims=True)
                x_two[row, :, part] = (slope_s[pl.ds(row, 1), part] * g).astype(BF16)

    for c in range(chunks - 1):
        first(c)
        tangents_here(c + 1)
    if gather:
        for j in range(1, nw):
            second_over(j)
    first(chunks - 1)

    w2 = whole(1)
    first_z = z == 0
    lap_two = bend_one * curv1_s[...] + jnp.where(first_z, slope_one * lapin_one, 0.0)
    vl_two = dot(jnp.concatenate([hidden_one.astype(BF16), halves(lap_two)], axis=0), w2)
    hidden_two = jnp.tanh(vl_two[:own] + b2)
    lapin_two = vl_two[own:2 * own] + vl_two[2 * own:]
    slope_two = 1.0 - hidden_two * hidden_two
    bend_two = -2.0 * hidden_two * slope_two
    weight_s[...] = readout * slope_two

    def second(c, carry):
        block = x_two[pl.ds(c * CHUNK, CHUNK)].reshape(CHUNK * cols, width)
        folded = [0.0] * CHUNK
        for part in parts:
            grad = dot(block, w2[:, part])
            for i in range(CHUNK):
                row = c * CHUNK + i
                g = grad[i * cols:(i + 1) * cols]
                curv2_s[pl.ds(row, 1), part] = jnp.sum(g * g, axis=0, keepdims=True)
                terms = weight_s[pl.ds(row, 1), part] * g
                folded[i] += sum(terms[:, j:j + 128] for j in range(0, terms.shape[1], 128))
        terms = jnp.concatenate(folded, axis=0)
        high = terms.astype(BF16)
        low = (terms - high.astype(F32)).astype(BF16)
        sums = dot(jnp.concatenate([high, low], axis=1), jnp.ones((256, 128), BF16))
        for i in range(CHUNK):
            here = walker_lane == c * CHUNK + i
            carry = carry + jnp.where(here, sums[i * cols:(i + 1) * cols], 0.0)
        return carry

    walker_lane = lax.broadcasted_iota(jnp.int32, (cols, 128), 1)
    columns = jnp.zeros((cols, 128), F32)
    for c in range(chunks):
        columns = second(c, columns)
    gradient = columns.T[:own]
    gbuf[...] = gradient

    send(gbuf, grad_out.at[mine, :], gs, gr, partner)
    keep = pltpu.make_async_copy(gbuf, grad_out.at[mine, :], loc.at[len(local)])
    keep.start()
    part = jnp.sum(
        readout * (slope_two * lapin_two + bend_two * curv2_s[...]), axis=1, keepdims=True
    ) + jnp.sum(gradient * gradient, axis=1, keepdims=True)
    amp = jnp.where(first_z, jnp.sum(readout * hidden_two, axis=1, keepdims=True), 0.0)
    lane = lax.broadcasted_iota(jnp.int32, (own, 128), 1)
    place = lane == lax.broadcasted_iota(jnp.int32, (own, 128), 0) + f * own
    kin_row = jnp.sum(jnp.where(place, part, 0.0), axis=0, keepdims=True)
    amp_row = jnp.sum(jnp.where(place, amp, 0.0), axis=0, keepdims=True)
    tile_row = lax.broadcasted_iota(jnp.int32, (8, 128), 0)
    msg[z, f] = jnp.where(tile_row == 0, amp_row, -0.5 * kin_row)
    slot = msg.at[z, f]
    others = [(k, g) for k in range(nz) for g in range(2) if k or g]
    for k, g in others:
        send(slot, slot, ms.at[k, g], mr.at[k, g], (w, z_at(k), other if g else f))
    for k, g in others:
        arrived(msg.at[z_at(k), other if g else f], ms.at[k, g], mr.at[k, g])
    total = msg[0, 0] + msg[0, 1]
    for k in range(1, nz):
        total = total + (msg[k, 0] + msg[k, 1])
    amp_out[...] = total[0:1, :2 * own]
    kin_out[...] = total[1:2, :2 * own]
    arrived(grad_out.at[theirs, :], gs, gr)
    keep.wait()
    for copy in sent:
        copy.wait_send()


def hand_over(*refs):
    sems = refs[-1]
    reads = [pltpu.make_async_copy(refs[i], refs[6 + i], sems.at[i]) for i in range(3)]
    writes = [pltpu.make_async_copy(refs[6 + i], refs[3 + i], sems.at[3 + i]) for i in range(3)]
    for copy in reads:
        copy.start()
    for read, write in zip(reads, writes):
        read.wait()
        write.start()
    for copy in writes:
        copy.wait()


def per_device(nw, nz, value_in, tang_in, lap_in, w_first, b_first, w_second, b_second, readout):
    walkers, cols, half = tang_in.shape
    width, own = 2 * half, walkers // 2
    shard = w_first.shape[0]
    gather = shard % 16 == 0
    if gather:
        w_shape = (nw, nz, 2, shard, width)
    else:
        w_shape = (width, width)
        w_first, w_second = (
            lax.all_gather(a, ("walker", "tangent", "feat"), axis=0, tiled=True) for a in (w_first, w_second)
        )
    chunks = own // CHUNK
    dma = pltpu.SemaphoreType.DMA
    in_hbm = pl.BlockSpec(memory_space=pltpu.HBM)
    in_vmem = pl.BlockSpec(memory_space=pltpu.VMEM)
    rows = own * cols
    row = jax.ShapeDtypeStruct((1, walkers), F32)
    results = pl.pallas_call(
        functools.partial(kernel, nw, nz, gather),
        out_shape=(jax.ShapeDtypeStruct((walkers, cols), F32), row, row),
        in_specs=[in_hbm] * 8,
        out_specs=(in_hbm, in_vmem, in_vmem),
        scratch_shapes=[
            pltpu.VMEM((own, cols, width), BF16),
            pltpu.VMEM((own, cols, width), BF16),
            pltpu.VMEM(w_shape, BF16),
            pltpu.VMEM(w_shape, BF16),
            pltpu.VMEM((2, own, width), BF16),
            pltpu.VMEM((3, 1, width), F32),
            pltpu.VMEM((own, width), F32),
            pltpu.VMEM((own, width), F32),
            pltpu.VMEM((own, width), F32),
            pltpu.VMEM((own, width), F32),
            pltpu.VMEM((own, cols), F32),
            pltpu.VMEM((nz, 2, 8, 128), F32),
            dma((8 + chunks,)),
            dma((2 + chunks,)),
            dma((2 + chunks,)),
            dma((2, nz)),
            dma((2, nz)),
            dma((nz, nw)),
            dma((nz, nw)),
            dma((nw,)),
            dma((nw,)),
            dma((nz,)),
            dma((nz,)),
            dma((nw,)),
            dma((nw,)),
            dma((nw,)),
            dma((nw,)),
            dma,
            dma,
            dma((nz, 2)),
            dma((nz, 2)),
        ],
        compiler_params=pltpu.CompilerParams(
            collective_id=0, has_side_effects=True, vmem_limit_bytes=64 * 2**20
        ),
        cost_estimate=pl.CostEstimate(
            flops=4 * rows * width * width, bytes_accessed=2 * rows * width, transcendentals=0
        ),
    )(
        value_in, tang_in, lap_in, w_first, b_first.reshape(1, width),
        w_second, b_second.reshape(1, width), readout.reshape(1, width),
    )
    grad, amp, kin = pl.pallas_call(
        hand_over,
        out_shape=[jax.ShapeDtypeStruct(a.shape, a.dtype) for a in results],
        in_specs=[in_hbm] * 3,
        out_specs=[in_hbm] * 3,
        scratch_shapes=[pltpu.VMEM(a.shape, a.dtype) for a in results] + [dma((6,))],
        compiler_params=pltpu.CompilerParams(vmem_limit_bytes=64 * 2**20),
    )(*results)
    return (amp.reshape(walkers), grad, kin.reshape(walkers))


def solution(mesh):
    placed = (
        P("walker", "feat"),
        P("walker", "tangent", "feat"),
        P("walker", "feat"),
        P(("walker", "tangent", "feat"), None),
        P(),
        P(("walker", "tangent", "feat"), None),
        P(),
        P(),
    )
    return jax.shard_map(
        functools.partial(per_device, mesh.shape["walker"], mesh.shape["tangent"]),
        mesh=mesh,
        in_specs=placed,
        out_specs=(P("walker"), P("walker", "tangent"), P("walker")),
        check_vma=False,
    )
```
